256 devices in a mesh: section: 32 (over z, y_lo, core), dp: 8 (over x, y_hi).
Axes of the slice: x: 4, y: 4 (y_hi: 2, y_lo: 2; y = y_hi * 2 + y_lo), z: 8, core: 2. Of those that a mesh axis runs over, the one named last changes fastest.
Arguments:
- entry_codes: bfloat16 [4, 128, 12288], P(None, 'dp', 'section'), may hold values from -16 to 16
- loss_target: bfloat16 [4, 128, 12288], P(None, 'dp', 'section'), may hold values from -6 to 6
- fwd_inflow: bfloat16 [32, 128, 12288], P('section', 'dp'), may hold values from -16 to 16
- bwd_inflow: bfloat16 [32, 128, 12288], P('section', 'dp'), may hold values from -16 to 16
- act_cache: bfloat16 [32, 32, 16, 12288], P('section', 'dp'), may hold values from -6 to 6
- act_exps: int32 [32, 32, 16, 96], P('section', 'dp'), may hold values from -5 to -1
- grad_cache: bfloat16 [32, 32, 16, 12288], P('section', 'dp'), may hold values from -6 to 6
- grad_exps: int32 [32, 32, 16, 96], P('section', 'dp'), may hold values from -5 to -1
- fwd_rows: int32 [32, 32], P('section', 'dp'), may hold values from 0 to 3, as said below
- bwd_rows: int32 [32, 32], P('section', 'dp'), may hold values from 0 to 3, as said below
- norm_gain: bfloat16 [32, 12288], P('section'), may hold values from 0.5 to 2
- w_in: bfloat16 [32, 64, 12288], P('section'), may hold values from -0.0546875 to 0.0546875
- w_out: bfloat16 [32, 64, 12288], P('section'), may hold values from -0.75 to 0.75
Outputs:
- grad_w_in: bfloat16 [32, 64, 12288], P('section', None, 'dp')
- grad_w_out: bfloat16 [32, 64, 12288], P('section', None, 'dp')
- grad_gain: float32 [32, 12288], P('section', 'dp')
- fwd_outflow: bfloat16 [32, 128, 12288], P('section', 'dp')
- bwd_outflow: bfloat16 [32, 128, 12288], P('section', 'dp')
The draws below stay inside these ranges and needn't reach their ends.
Inputs may be any that keep to these rules, and one draw needn't show every extreme that they name: `fwd_rows`: each aligned block of 4 entries (one section, one data replica) names every row 0 to 3 once. `bwd_rows`: each aligned block of 4 entries (one section, one data replica) names every row 0 to 3 once.
All inputs are finite; a program needn't handle non-finite values.
Results may differ from the reference program's by a relative error of at most 0.017.
Values may be sent and summed in bfloat16 or wider, within the bound.
A program may use at most 128 MiB of HBM per device.

```python
import math
import jax
import jax.numpy as jnp
from jax import lax

D = 12288
WIN = 64
ROWS = 16
TICKS = 4
SECTIONS = 32
BATCH_ROWS = 128
CACHED = 32
BLOCKS = 96
N_DP = 8


def draw_fwd_rows(key, part):
    key = jax.random.fold_in(key, 11)
    keys = jax.random.split(key, SECTIONS * N_DP)
    orders = jax.vmap(lambda one: jax.random.permutation(one, TICKS))(keys)
    return orders.reshape((SECTIONS, N_DP * TICKS)).astype(jnp.int32)


def draw_bwd_rows(key, part):
    key = jax.random.fold_in(key, 23)
    keys = jax.random.split(key, SECTIONS * N_DP)
    orders = jax.vmap(lambda one: jax.random.permutation(one, TICKS))(keys)
    return orders.reshape((SECTIONS, N_DP * TICKS)).astype(jnp.int32)


def plant(values, stream_key, smallest, high):
    spot = [jax.random.randint(jax.random.fold_in(stream_key, axis), (), 0, length) for axis, length in enumerate(values.shape)]
    longest = values.shape.index(max(values.shape))
    next_to = spot[:longest] + [(spot[longest] + 1) % values.shape[longest]] + spot[longest + 1:]
    return values.at[tuple(spot)].set(smallest).at[tuple(next_to)].set(high)


def block_scale(stream_key, shape, pieces, least, top_value):
    factor_of = 1.0
    for axis_at, shards_of in pieces:
        heights = jax.random.uniform(jax.random.fold_in(jax.random.fold_in(stream_key, 6), axis_at), (shards_of,), jnp.float32, least / len(pieces), top_value / len(pieces))
        factor_of = factor_of * jnp.repeat(jnp.exp(heights), shape[axis_at] // shards_of).reshape((-1,) + (1,) * (len(shape) - 1 - axis_at))
    return factor_of


def bell_draw(own_key, shape, spread, bound, cuts=(), held_as=jnp.bfloat16):
    factor_of = block_scale(own_key, shape, cuts, -0.22, 0.18) if cuts else 1.0
    result = jax.random.normal(own_key, shape, jnp.float32) * spread * factor_of
    return jnp.minimum(jnp.maximum(result, -bound), bound).astype(held_as)


def setup_inputs(seed: int = 0) -> dict:
    key_list = jax.random.split(jax.random.key(seed), 14)
    return {
        "entry_codes": jnp.clip(jax.random.uniform(key_list[0], (TICKS, BATCH_ROWS, D), jnp.float32, -16.0, 16.0) * block_scale(key_list[0], (TICKS, BATCH_ROWS, D), ((1, 8), (2, 32)), -0.4, 0.0), -16.0, 16.0).astype(jnp.bfloat16),
        "loss_target": bell_draw(key_list[1], (TICKS, BATCH_ROWS, D), 1.0, 6.0, ((1, 8), (2, 32))),
        "fwd_inflow": jnp.clip(jax.random.uniform(key_list[2], (SECTIONS, BATCH_ROWS, D), jnp.float32, -16.0, 16.0) * block_scale(key_list[2], (SECTIONS, BATCH_ROWS, D), ((0, 32), (1, 8)), -0.4, 0.0), -16.0, 16.0).astype(jnp.bfloat16),
        "bwd_inflow": jnp.clip(jax.random.uniform(key_list[3], (SECTIONS, BATCH_ROWS, D), jnp.float32, -16.0, 16.0) * block_scale(key_list[3], (SECTIONS, BATCH_ROWS, D), ((0, 32), (1, 8)), -0.4, 0.0), -16.0, 16.0).astype(jnp.bfloat16),
        "act_cache": bell_draw(key_list[4], (SECTIONS, CACHED, ROWS, D), 1.0, 6.0, ((0, 32), (1, 8))),
        "act_exps": plant(jax.random.randint(key_list[5], (SECTIONS, CACHED, ROWS, BLOCKS), -5, 0), jax.random.fold_in(key_list[5], 1), -5, -1).astype(jnp.int32),
        "grad_cache": bell_draw(key_list[6], (SECTIONS, CACHED, ROWS, D), 1.0, 6.0, ((0, 32), (1, 8))),
        "grad_exps": plant(jax.random.randint(key_list[7], (SECTIONS, CACHED, ROWS, BLOCKS), -5, 0), jax.random.fold_in(key_list[7], 1), -5, -1).astype(jnp.int32),
        "fwd_rows": draw_fwd_rows(jax.random.fold_in(key_list[13], 71), 0),
        "bwd_rows": draw_bwd_rows(jax.random.fold_in(key_list[13], 71), 0),
        "norm_gain": jnp.clip(jnp.exp(math.log(2.0) - 1.3862944 * jax.random.uniform(key_list[10], (SECTIONS, D), jnp.float32) ** block_scale(key_list[10], (SECTIONS, D), ((0, 32),), -0.2, 0.2)), 0.5, 2.0).astype(jnp.bfloat16),
        "w_in": bell_draw(key_list[11], (SECTIONS, WIN, D), D ** -0.5, 0.0546875, ((0, 32),)),
        "w_out": bell_draw(key_list[12], (SECTIONS, WIN, D), WIN ** -0.5, 0.75, ((0, 32),)),
    }


code_limit = 16.0

def blocks(values, scale):
    shaped = values.reshape(values.shape[:-1] + (scale.shape[-1], 128))
    return (shaped * scale[..., None]).reshape(values.shape)

def decode(cached, scale, code):
    return (cached.astype(jnp.float32) + blocks(code.astype(jnp.float32), scale)).astype(jnp.bfloat16)

def encode(values, cached, inverse):
    moved = blocks(values - cached.astype(jnp.float32), inverse)
    return jnp.clip(moved, -code_limit, code_limit).astype(jnp.bfloat16)

def gelu_slope(preactivation):
    return 0.5 * (1.0 + jax.scipy.special.erf(preactivation * 0.7071067811865476)) + preactivation * jnp.exp(-0.5 * preactivation * preactivation) * 0.3989422804014327

def layer_pieces(layer_in, gain_vector, first_weight, second_weight):
    input_float = layer_in.astype(jnp.float32)
    inverse_root_mean = lax.rsqrt(lax.optimization_barrier(jnp.mean(input_float * input_float, axis=-1, keepdims=True)) + 1e-05)
    normalized_input = input_float * inverse_root_mean
    normalized_rows = (normalized_input * gain_vector[:, None, None, :]).astype(jnp.bfloat16)
    preactivation = jnp.einsum('sprd,shd->sprh', normalized_rows.astype(jnp.float32), first_weight)
    active_rows = jax.nn.gelu(preactivation, approximate=False).astype(jnp.bfloat16)
    layer_output = input_float + jnp.einsum('sprh,shd->sprd', active_rows.astype(jnp.float32), second_weight)
    return (layer_output, inverse_root_mean, normalized_input, normalized_rows, preactivation, active_rows)

def pick_rows(cache, exps, rows):
    shaped = cache.reshape((SECTIONS, N_DP, TICKS, ROWS, D))
    powers = exps.reshape((SECTIONS, N_DP, TICKS, ROWS, D // 128))
    order = rows.reshape((SECTIONS, N_DP, TICKS)).astype(jnp.int32)
    chosen = jnp.take_along_axis(shaped, order[:, :, :, None, None], axis=2)
    power = jnp.take_along_axis(powers, order[:, :, :, None, None], axis=2).astype(jnp.float32)
    return (chosen, jnp.exp2(power), jnp.exp2(-power))

def reference(entry_codes, loss_target, fwd_inflow, bwd_inflow, act_cache, act_exps, grad_cache, grad_exps, fwd_rows, bwd_rows, norm_gain, w_in, w_out):
    acts, act_scale, act_inv = pick_rows(act_cache, act_exps, fwd_rows)
    stored = pick_rows(act_cache, act_exps, bwd_rows)[0]
    grads, grad_scale, grad_inv = pick_rows(grad_cache, grad_exps, bwd_rows)
    next_acts = jnp.concatenate([acts[1:], jnp.zeros_like(acts[:1])], axis=0)
    next_inv = jnp.concatenate([act_inv[1:], jnp.zeros_like(act_inv[:1])], axis=0)
    prev_grads = jnp.concatenate([jnp.zeros_like(grads[:1]), grads[:-1]], axis=0)
    prev_inv = jnp.concatenate([jnp.zeros_like(grad_inv[:1]), grad_inv[:-1]], axis=0)
    entries = entry_codes.reshape((TICKS, N_DP, ROWS, D))
    targets = loss_target.reshape((TICKS, N_DP, ROWS, D))
    fwd_recv = fwd_inflow.reshape((SECTIONS, N_DP, ROWS, D))
    bwd_recv = bwd_inflow.reshape((SECTIONS, N_DP, ROWS, D))
    section_ids = jnp.arange(SECTIONS)[:, None, None, None]
    first = section_ids == 0
    last = section_ids == SECTIONS - 1
    gain_vector = norm_gain.astype(jnp.float32)
    first_weight = w_in.astype(jnp.float32)
    second_weight = w_out.astype(jnp.float32)
    zero_row = jnp.zeros((1, N_DP, ROWS, D), jnp.bfloat16)
    sum_first = jnp.zeros((SECTIONS, WIN, D), jnp.float32)
    sum_second = jnp.zeros((SECTIONS, WIN, D), jnp.float32)
    gain_gradient_sum = jnp.zeros((SECTIONS, D), jnp.float32)
    fwd_last = None
    bwd_last = None
    for tick in range(TICKS):
        code = jnp.where(first, entries[tick][None], fwd_recv)
        layer_in = decode(acts[:, :, tick], act_scale[:, :, tick], code)
        layer_output = layer_pieces(layer_in, gain_vector, first_weight, second_weight)[0]
        if tick < TICKS - 1:
            sent = encode(layer_output, next_acts[:, :, tick + 1], next_inv[:, :, tick + 1])
            fwd_recv = jnp.concatenate([zero_row, sent[:-1]], axis=0)
        else:
            fwd_last = layer_output.astype(jnp.bfloat16)
        loss_grad = (layer_output - targets[tick][None].astype(jnp.float32)).astype(jnp.bfloat16)
        grad_in = jnp.where(last, loss_grad, decode(grads[:, :, tick], grad_scale[:, :, tick], bwd_recv))
        backward_input = jnp.where(last, layer_in, stored[:, :, tick])
        unused_slot, inverse_root_mean, normalized_input, normalized_rows, preactivation, active_rows = layer_pieces(backward_input, gain_vector, first_weight, second_weight)
        gain_float = grad_in.astype(jnp.float32)
        d_active = jnp.einsum('sprd,shd->sprh', gain_float, second_weight)
        d_pre = (d_active * gelu_slope(preactivation)).astype(jnp.bfloat16)
        norm_gradient = jnp.einsum('sprh,shd->sprd', d_pre.astype(jnp.float32), first_weight)
        sum_first = sum_first + jnp.einsum('sprh,sprd->shd', d_pre.astype(jnp.float32), normalized_rows.astype(jnp.float32))
        sum_second = sum_second + jnp.einsum('sprh,sprd->shd', active_rows.astype(jnp.float32), gain_float)
        gain_gradient_sum = gain_gradient_sum + lax.optimization_barrier(jnp.sum(norm_gradient * normalized_input, axis=(1, 2)))
        scaled_rows = norm_gradient * gain_vector[:, None, None, :]
        input_gradient = gain_float + inverse_root_mean * (scaled_rows - normalized_input * lax.optimization_barrier(jnp.mean(scaled_rows * normalized_input, axis=-1, keepdims=True)))
        if tick < TICKS - 1:
            sent_back = encode(input_gradient, prev_grads[:, :, tick + 1], prev_inv[:, :, tick + 1])
            bwd_recv = jnp.concatenate([sent_back[1:], zero_row], axis=0)
        else:
            bwd_last = input_gradient.astype(jnp.bfloat16)
    factor = 1.0 / (TICKS * N_DP)
    grad_w_in = (sum_first * factor).astype(jnp.bfloat16)
    grad_w_out = (sum_second * factor).astype(jnp.bfloat16)
    grad_gain = gain_gradient_sum * factor
    fwd_outflow = fwd_last.reshape((SECTIONS, N_DP * ROWS, D))
    bwd_outflow = bwd_last.reshape((SECTIONS, N_DP * ROWS, D))
    return (grad_w_in, grad_w_out, grad_gain, fwd_outflow, bwd_outflow)
```

```python
import functools

import jax
import jax.numpy as jnp
from jax import lax
from jax.experimental import pallas as pl
from jax.experimental.pallas import tpu as pltpu
from jax.sharding import PartitionSpec as P

MESH = pl.DeviceIdType.MESH
ROWS = 16
TICKS = 4
F32 = jnp.float32
BF16 = jnp.bfloat16


def dot_last(a, b):
    return lax.dot_general(a, b, (((1,), (1,)), ((), ())), preferred_element_type=F32)


def dot_first(a, b):
    return lax.dot_general(a, b, (((0,), (0,)), ((), ())), preferred_element_type=F32)


def dot_plain(a, b):
    return lax.dot_general(a, b, (((1,), (0,)), ((), ())), preferred_element_type=F32)


def half_erf(u):
    return 0.5 * (1.0 + lax.erf(u * 0.7071067811865476))


def gelu(u):
    return u * half_erf(u)


def gelu_slope(u):
    return half_erf(u) + u * jnp.exp(-0.5 * u * u) * 0.3989422804014327


def kernel(
    sections,
    replicas,
    fwd_rows,
    bwd_rows,
    gain_ref,
    act_exps,
    grad_exps,
    entry_hbm,
    target_hbm,
    fwd_inflow,
    bwd_inflow,
    act_hbm,
    grad_hbm,
    w_in_hbm,
    w_out_hbm,
    gw_in_out,
    gw_out_out,
    ggain_out,
    fwd_out,
    bwd_out,
    act,
    grad,
    w_in,
    w_out,
    wg,
    fwd_code,
    bwd_code,
    entries,
    targets,
    lim_act,
    lim_grad,
    x_back,
    x_now,
    g_all,
    y_send,
    y_recv,
    d_send,
    d_recv,
    u_back,
    r_back,
    a_back,
    du_tick,
    factors,
    x_gather,
    g_gather,
    f_gather,
    p_send,
    p_recv,
    load_sem,
    entry_send,
    entry_recv,
    y_send_sem,
    y_recv_sem,
    d_send_sem,
    d_recv_sem,
    x_send_sem,
    x_recv_sem,
    g_send_sem,
    g_recv_sem,
    f_send_sem,
    f_recv_sem,
    p_send_sem,
    p_recv_sem,
    out_sem,
):
    width = w_in.shape[1]
    ring = replicas // 2
    cut = width // ring
    share = width // replicas
    piece = width // sections
    inv_width = 1.0 / width
    s = lax.axis_index("section")
    p = lax.axis_index("dp")
    px = p // 2
    py = p % 2
    first = s == 0
    last = s == sections - 1
    not_first = s > 0
    not_last = s < sections - 1
    mate = px * 2 + (1 - py)

    barrier = pltpu.get_barrier_semaphore()

    def greet(where):
        pl.semaphore_signal(barrier, inc=1, device_id=where, device_id_type=MESH)

    @pl.when(not_first)
    def _():
        greet({"section": s - 1})

    @pl.when(not_last)
    def _():
        greet({"section": s + 1})

    for k in range(1, ring):
        greet({"dp": lax.rem(px + k, ring) * 2 + py})
    greet({"dp": mate})

    @pl.when(first)
    def _():
        def tell(i, c):
            greet({"section": i})
            return c

        lax.fori_loop(1, sections, tell, 0)

    @pl.when(last)
    def _():
        def tell(i, c):
            greet({"section": i})
            return c

        lax.fori_loop(0, sections - 1, tell, 0)

    loads = [
        pltpu.make_async_copy(src, dst, load_sem.at[i])
        for i, (src, dst) in enumerate(
            [
                (act_hbm, act),
                (w_in_hbm, w_in),
                (fwd_inflow, fwd_code),
                (w_out_hbm, w_out),
                (grad_hbm, grad),
                (bwd_inflow, bwd_code),
                (act_hbm, x_back),
            ]
        )
    ]
    for load in loads[:6]:
        load.start()

    @pl.when(not_last)
    def _():
        loads[6].start()

    count = (
        jnp.where(not_first, 2, 0) + jnp.where(not_last, 2, 0) + (ring - 1) + 1
    )
    pl.semaphore_wait(barrier, count)

    mine = pl.ds(pl.multiple_of(s * piece, 128), piece)

    def entry_copy(which, t):
        src = (entry_hbm, target_hbm)[which]
        dst = (entries, targets)[which]
        return pltpu.make_async_remote_copy(
            src_ref=src.at[t],
            dst_ref=dst.at[t, :, mine],
            send_sem=entry_send.at[which, t],
            recv_sem=entry_recv.at[which, t],
            device_id={"section": (0, sections - 1)[which]},
            device_id_type=MESH,
        )

    def entry_local(which, t):
        src = (entry_hbm, target_hbm)[which]
        dst = (entries, targets)[which]
        return pltpu.make_async_copy(
            src.at[t], dst.at[t, :, mine], entry_recv.at[which, t]
        )

    def entry_wait(which, t):
        dst = (entries, targets)[which]
        pltpu.make_async_copy(dst.at[t], dst.at[t], entry_recv.at[which, t]).wait()

    for t in range(TICKS):
        for which, away, here in ((0, not_first, first), (1, not_last, last)):

            @pl.when(away)
            def _():
                entry_copy(which, t).start()

            @pl.when(here)
            def _():
                entry_local(which, t).start()

    def columns(j):
        return pl.ds(pl.multiple_of(j * cut, 128), cut)

    def spread(src, dst, send_sem, recv_sem, slot, j):
        @pl.when(j != px)
        def _():
            pltpu.make_async_remote_copy(
                src_ref=src.at[slot, :, columns(j)],
                dst_ref=dst.at[px, slot],
                send_sem=send_sem.at[slot, j],
                recv_sem=recv_sem.at[px, slot],
                device_id={"dp": j * 2 + py},
                device_id_type=MESH,
            ).start()

        @pl.when(j == px)
        def _():
            pltpu.make_async_copy(
                src.at[slot, :, columns(j)], dst.at[px, slot], recv_sem.at[px, slot]
            ).start()

    def spread_wait(src, dst, send_sem, recv_sem):
        def one(i, c):
            k, slot = i // TICKS, i % TICKS

            @pl.when(k != px)
            def _():
                copy = pltpu.make_async_remote_copy(
                    src_ref=src.at[slot, :, columns(k)],
                    dst_ref=dst.at[k, slot],
                    send_sem=send_sem.at[slot, k],
                    recv_sem=recv_sem.at[k, slot],
                    device_id={"dp": k * 2 + py},
                    device_id_type=MESH,
                )
                copy.wait_recv()
                copy.wait_send()

            @pl.when(k == px)
            def _():
                pltpu.make_async_copy(
                    src.at[slot, :, columns(k)], dst.at[k, slot], recv_sem.at[k, slot]
                ).wait()

            return c

        lax.fori_loop(0, ring * TICKS, one, 0)

    def x_spread(slot, j):
        spread(x_back, x_gather, x_send_sem, x_recv_sem, slot, j)

    def g_spread(slot, j):
        spread(g_all, g_gather, g_send_sem, g_recv_sem, slot, j)

    @pl.when(not_last)
    def _():
        loads[6].wait()
        for slot in range(TICKS):
            for k in range(ring):
                x_spread(slot, lax.rem(px + k, ring))

    blocks = act_exps.shape[-1]
    group = min(8, blocks)
    wide = group * 128
    powers = jnp.concatenate(
        [
            act_exps[...].reshape(TICKS * ROWS, blocks),
            grad_exps[...].reshape(TICKS * ROWS, blocks),
        ],
        axis=0,
    ).astype(F32)
    scales = jnp.exp2(powers + 4.0).astype(BF16)

    def expand(j, c):
        at = pl.ds(pl.multiple_of(j * wide, 128), wide)
        row = lax.broadcasted_iota(jnp.int32, (blocks, wide), 0)
        col = lax.broadcasted_iota(jnp.int32, (blocks, wide), 1)
        pick = jnp.where(row == j * group + col // 128, 1.0, 0.0).astype(BF16)
        both = dot_plain(scales, pick).astype(BF16)
        lim_act[:, :, at] = both[: TICKS * ROWS].reshape(TICKS, ROWS, wide)
        lim_grad[:, :, at] = both[TICKS * ROWS :].reshape(TICKS, ROWS, wide)
        return c

    lax.fori_loop(0, blocks // group, expand, 0)

    loads[1].wait()

    def fold(j, c):
        wg[:, columns(j)] = (
            w_in[:, columns(j)].astype(F32) * gain_ref[:, columns(j)].astype(F32)
        ).astype(BF16)
        return c

    lax.fori_loop(0, ring, fold, 0)
    loads[0].wait()
    loads[2].wait()
    loads[3].wait()

    def y_copy(t, j):
        return pltpu.make_async_remote_copy(
            src_ref=y_send.at[t, :, columns(j)],
            dst_ref=y_recv.at[t, :, columns(j)],
            send_sem=y_send_sem.at[t, j],
            recv_sem=y_recv_sem.at[t, j],
            device_id={"section": s + 1},
            device_id_type=MESH,
        )

    def d_copy(t, j):
        return pltpu.make_async_remote_copy(
            src_ref=d_send.at[t, :, columns(j)],
            dst_ref=d_recv.at[t, :, columns(j)],
            send_sem=d_send_sem.at[t, j],
            recv_sem=d_recv_sem.at[t, j],
            device_id={"section": s - 1},
            device_id_type=MESH,
        )

    def scaled(cache, limit, code):
        return (
            cache.astype(F32) + limit.astype(F32) * 0.0625 * code.astype(F32)
        ).astype(BF16)

    def clipped(cache, limit, value):
        cache, limit, value = cache.astype(F32), limit.astype(F32), value.astype(F32)
        return jnp.minimum(jnp.maximum(value, cache - limit), cache + limit).astype(BF16)

    def forward(t):
        row = fwd_rows[0, t]

        @pl.when(first)
        def _():
            entry_wait(0, t)

        def take(j, c):
            total, u = c
            at = columns(j)
            cache, limit = act[row, :, at], lim_act[row, :, at]
            if t == 0:

                @pl.when(first)
                def _():
                    x_now[:, at] = scaled(cache, limit, entries[t, :, at])

                @pl.when(not_first)
                def _():
                    x_now[:, at] = scaled(cache, limit, fwd_code[:, at])

            else:

                @pl.when(first)
                def _():
                    x_now[:, at] = scaled(cache, limit, entries[t, :, at])

                @pl.when(not_first)
                def _():
                    y_copy(t - 1, j).wait_recv()
                    x_now[:, at] = clipped(cache, limit, y_recv[t - 1, :, at])

            x = x_now[:, at]
            xf = x.astype(F32)
            total = total + jnp.sum(xf * xf, axis=1, keepdims=True)
            u = u + dot_last(x, wg[:, at])

            @pl.when(last)
            def _():
                x_back[t, :, at] = x
                x_spread(t, j)

            return total, u

        total, u = lax.fori_loop(
            0,
            ring,
            take,
            (jnp.zeros((ROWS, 1), F32), jnp.zeros((ROWS, w_in.shape[0]), F32)),
        )
        r = lax.rsqrt(total * inv_width + 1e-05)
        u = u * r
        a = gelu(u).astype(BF16)

        @pl.when(last)
        def _():
            u_back[t] = u
            r_back[t] = jnp.broadcast_to(r, (ROWS, 128))
            a_back[t] = a
            entry_wait(1, t)

        def give(j, c):
            at = columns(j)
            y = x_now[:, at].astype(F32) + dot_plain(a, w_out[:, at])
            y_send[t, :, at] = y.astype(BF16)
            if t < TICKS - 1:

                @pl.when(not_last)
                def _():
                    y_copy(t, j).start()

            @pl.when(last)
            def _():
                g_all[t, :, at] = (y - targets[t, :, at].astype(F32)).astype(BF16)

            return c

        lax.fori_loop(0, ring, give, 0)
        if t == TICKS - 1:
            pltpu.make_async_copy(y_send.at[t], fwd_out, out_sem.at[0]).start()

    def prepare_backward():
        def take(j, c):
            total, u = c
            at = columns(j)
            x = x_back[:, :, at].reshape(TICKS * ROWS, cut)
            xf = x.astype(F32)
            return (
                total + jnp.sum(xf * xf, axis=1, keepdims=True),
                u + dot_last(x, wg[:, at]),
            )

        total, u = lax.fori_loop(
            0,
            ring,
            take,
            (
                jnp.zeros((TICKS * ROWS, 1), F32),
                jnp.zeros((TICKS * ROWS, w_in.shape[0]), F32),
            ),
        )
        r = lax.rsqrt(total * inv_width + 1e-05)
        u = u * r
        u_back[...] = u.reshape(u_back.shape)
        r_back[...] = jnp.broadcast_to(r, (TICKS * ROWS, 128)).reshape(r_back.shape)
        a_back[...] = gelu(u).astype(BF16).reshape(a_back.shape)

    def backward(t):
        row = bwd_rows[0, t]
        used = jnp.where(last, t, row)

        def take(j, c):
            at = columns(j)

            @pl.when(not_last)
            def _():
                cache, limit = grad[row, :, at], lim_grad[row, :, at]
                if t == 0:
                    g_all[t, :, at] = scaled(cache, limit, bwd_code[:, at])
                else:
                    d_copy(t - 1, j).wait_recv()
                    g_all[t, :, at] = clipped(cache, limit, d_recv[t - 1, :, at])

            g_spread(t, j)
            return c + dot_last(g_all[t, :, at], w_out[:, at])

        d_active = lax.fori_loop(
            0, ring, take, jnp.zeros((ROWS, w_in.shape[0]), F32)
        )
        u = u_back[used]
        r = r_back[used][:, :1]
        du = d_active * gelu_slope(u)
        shift = r * r * (jnp.sum(du * u, axis=1, keepdims=True) * inv_width)
        du_tick[t] = (du * r).astype(BF16)
        factors[1, t] = a_back[used]
        du = du.astype(BF16)

        def give(j, c):
            at = columns(j)
            dx = (
                g_all[t, :, at].astype(F32)
                + r * dot_plain(du, wg[:, at])
                - x_back[used, :, at].astype(F32) * shift
            )
            d_send[t, :, at] = dx.astype(BF16)
            if t < TICKS - 1:

                @pl.when(not_first)
                def _():
                    d_copy(t, j).start()

            return c

        lax.fori_loop(0, ring, give, 0)
        if t == TICKS - 1:
            pltpu.make_async_copy(d_send.at[t], bwd_out, out_sem.at[1]).start()

    def factor_copy(to, frm):
        return pltpu.make_async_remote_copy(
            src_ref=factors,
            dst_ref=f_gather.at[frm],
            send_sem=f_send_sem.at[to],
            recv_sem=f_recv_sem.at[frm],
            device_id={"dp": to * 2 + py},
            device_id_type=MESH,
        )

    forward(0)
    loads[4].wait()
    loads[5].wait()

    @pl.when(not_last)
    def _():
        prepare_backward()

    backward(0)
    for t in range(1, TICKS):
        forward(t)
        backward(t)

    used = [jnp.where(last, t, bwd_rows[0, t]) for t in range(TICKS)]
    for q in range(TICKS):
        at = 0
        for t in range(1, TICKS):
            at = jnp.where(used[t] == q, t, at)
        factors[0, q] = du_tick[at]
    for k in range(1, ring):
        factor_copy(lax.rem(px + k, ring), px).start()
    own = pltpu.make_async_copy(factors, f_gather.at[px], f_recv_sem.at[px])
    own.start()
    spread_wait(x_back, x_gather, x_send_sem, x_recv_sem)
    spread_wait(g_all, g_gather, g_send_sem, g_recv_sem)
    own.wait()
    for k in range(1, ring):
        other = lax.rem(px + k, ring)
        factor_copy(other, other).wait()

    rows = ring * TICKS * ROWS
    win = w_in.shape[0]
    du_rows = f_gather[:, 0].reshape(rows, win)
    a_rows = f_gather[:, 1].reshape(rows, win)

    def products(half):
        at = pl.ds(pl.multiple_of(half * share, 128), share)
        return (
            dot_first(du_rows, x_gather[:, :, :, at].reshape(rows, share)),
            dot_first(a_rows, g_gather[:, :, :, at].reshape(rows, share)),
        )

    in_part, out_part = products(1 - py)
    p_send[0] = in_part.astype(BF16)
    p_send[1] = out_part.astype(BF16)
    swap = pltpu.make_async_remote_copy(
        src_ref=p_send,
        dst_ref=p_recv,
        send_sem=p_send_sem,
        recv_sem=p_recv_sem,
        device_id={"dp": mate},
        device_id_type=MESH,
    )
    swap.start()
    in_part, out_part = products(py)
    swap.wait()
    in_part = in_part + p_recv[0].astype(F32)
    out_part = out_part + p_recv[1].astype(F32)
    factor = 1.0 / (TICKS * replicas)
    at = pl.ds(pl.multiple_of(p * share, 128), share)
    gw_in_out[...] = (in_part * (gain_ref[:, at].astype(F32) * factor)).astype(BF16)
    gw_out_out[...] = (out_part * factor).astype(BF16)
    ggain_out[...] = (
        jnp.sum(in_part * w_in[:, at].astype(F32), axis=0, keepdims=True) * factor
    )

    for t in range(TICKS):

        @pl.when(not_first)
        def _():
            entry_copy(0, t).wait_send()

        @pl.when(not_last)
        def _():
            entry_copy(1, t).wait_send()

    for t in range(TICKS - 1):
        for j in range(ring):

            @pl.when(not_last)
            def _():
                y_copy(t, j).wait_send()

            @pl.when(not_first)
            def _():
                d_copy(t, j).wait_send()

    pltpu.make_async_copy(y_send.at[TICKS - 1], fwd_out, out_sem.at[0]).wait()
    pltpu.make_async_copy(d_send.at[TICKS - 1], bwd_out, out_sem.at[1]).wait()


def solution(mesh):
    sections = mesh.shape["section"]
    replicas = mesh.shape["dp"]

    def body(
        entry_codes,
        loss_target,
        fwd_inflow,
        bwd_inflow,
        act_cache,
        act_exps,
        grad_cache,
        grad_exps,
        fwd_rows,
        bwd_rows,
        norm_gain,
        w_in,
        w_out,
    ):
        win, width = w_in.shape[1:]
        ring = replicas // 2
        cut = width // ring
        share = width // replicas
        blocks = act_exps.shape[-1]
        full = (ROWS, width)
        dma = pltpu.SemaphoreType.DMA
        hbm = pl.BlockSpec(memory_space=pl.ANY)
        vmem = pl.BlockSpec(memory_space=pltpu.VMEM)
        smem = pl.BlockSpec(memory_space=pltpu.SMEM)
        outs = pl.pallas_call(
            functools.partial(kernel, sections, replicas),
            out_shape=(
                jax.ShapeDtypeStruct((win, share), BF16),
                jax.ShapeDtypeStruct((win, share), BF16),
                jax.ShapeDtypeStruct((1, share), F32),
                jax.ShapeDtypeStruct(full, BF16),
                jax.ShapeDtypeStruct(full, BF16),
            ),
            in_specs=[smem, smem, vmem, vmem, vmem] + [hbm] * 8,
            out_specs=(vmem, vmem, vmem, hbm, hbm),
            scratch_shapes=[
                pltpu.VMEM((TICKS,) + full, BF16),
                pltpu.VMEM((TICKS,) + full, BF16),
                pltpu.VMEM((win, width), BF16),
                pltpu.VMEM((win, width), BF16),
                pltpu.VMEM((win, width), BF16),
                pltpu.VMEM(full, BF16),
                pltpu.VMEM(full, BF16),
                pltpu.VMEM((TICKS,) + full, BF16),
                pltpu.VMEM((TICKS,) + full, BF16),
                pltpu.VMEM((TICKS,) + full, BF16),
                pltpu.VMEM((TICKS,) + full, BF16),
                pltpu.VMEM((TICKS,) + full, BF16),
                pltpu.VMEM(full, BF16),
                pltpu.VMEM((TICKS,) + full, BF16),
                pltpu.VMEM((TICKS,) + full, BF16),
                pltpu.VMEM((TICKS - 1,) + full, BF16),
                pltpu.VMEM((TICKS,) + full, BF16),
                pltpu.VMEM((TICKS - 1,) + full, BF16),
                pltpu.VMEM((TICKS, ROWS, win), F32),
                pltpu.VMEM((TICKS, ROWS, 128), F32),
                pltpu.VMEM((TICKS, ROWS, win), BF16),
                pltpu.VMEM((TICKS, ROWS, win), BF16),
                pltpu.VMEM((2, TICKS, ROWS, win), BF16),
                pltpu.VMEM((ring, TICKS, ROWS, cut), BF16),
                pltpu.VMEM((ring, TICKS, ROWS, cut), BF16),
                pltpu.VMEM((ring, 2, TICKS, ROWS, win), BF16),
                pltpu.VMEM((2, win, share), BF16),
                pltpu.VMEM((2, win, share), BF16),
                dma((7,)),
                dma((2, TICKS)),
                dma((2, TICKS)),
                dma((TICKS - 1, ring)),
                dma((TICKS - 1, ring)),
                dma((TICKS - 1, ring)),
                dma((TICKS - 1, ring)),
                dma((TICKS, ring)),
                dma((ring, TICKS)),
                dma((TICKS, ring)),
                dma((ring, TICKS)),
                dma((ring,)),
                dma((ring,)),
                dma,
                dma,
                dma((2,)),
            ],
            compiler_params=pltpu.CompilerParams(
                collective_id=0,
                has_side_effects=True,
                vmem_limit_bytes=48 * 1024 * 1024,
            ),
        )(
            fwd_rows,
            bwd_rows,
            norm_gain,
            act_exps[0],
            grad_exps[0],
            entry_codes,
            loss_target,
            fwd_inflow[0],
            bwd_inflow[0],
            act_cache[0],
            grad_cache[0],
            w_in[0],
            w_out[0],
        )
        gw_in, gw_out, ggain, fwd_last, bwd_last = outs
        return gw_in[None], gw_out[None], ggain, fwd_last[None], bwd_last[None]

    return jax.shard_map(
        body,
        mesh=mesh,
        in_specs=(
            P(None, "dp", "section"),
            P(None, "dp", "section"),
            P("section", "dp", None),
            P("section", "dp", None),
            P("section", "dp", None, None),
            P("section", "dp", None, None),
            P("section", "dp", None, None),
            P("section", "dp", None, None),
            P("section", "dp"),
            P("section", "dp"),
            P("section", None),
            P("section", None, None),
            P("section", None, None),
        ),
        out_specs=(
            P("section", None, "dp"),
            P("section", None, "dp"),
            P("section", "dp"),
            P("section", "dp", None),
            P("section", "dp", None),
        ),
        check_vma=False,
    )
```

```python
import functools

import jax
import jax.numpy as jnp
from jax import lax
from jax.experimental import pallas as pl
from jax.experimental.pallas import tpu as pltpu
from jax.sharding import PartitionSpec as P

MESH = pl.DeviceIdType.MESH
ROWS = 16
TICKS = 4
VMEM_BYTES = 64 * 1024 * 1024
F32 = jnp.float32
BF16 = jnp.bfloat16


def dot_last(a, b):
    return lax.dot_general(a, b, (((1,), (1,)), ((), ())), preferred_element_type=F32)


def dot_first(a, b):
    return lax.dot_general(a, b, (((0,), (0,)), ((), ())), preferred_element_type=F32)


def dot_plain(a, b):
    return lax.dot_general(a, b, (((1,), (0,)), ((), ())), preferred_element_type=F32)


def half_erf(u):
    return 0.5 * (1.0 + lax.erf(u * 0.7071067811865476))


def gelu(u):
    return u * half_erf(u)


def gelu_slope(u):
    return half_erf(u) + u * jnp.exp(-0.5 * u * u) * 0.3989422804014327


def kernel(
    sections,
    replicas,
    fwd_rows_hbm,
    bwd_rows_hbm,
    gain_hbm,
    act_exps_hbm,
    grad_exps_hbm,
    entry_hbm,
    target_hbm,
    fwd_inflow,
    bwd_inflow,
    act_hbm,
    grad_hbm,
    w_in_hbm,
    w_out_hbm,
    gw_in_out,
    gw_out_out,
    ggain_out,
    fwd_out,
    bwd_out,
    fwd_rows,
    bwd_rows,
    gain_ref,
    act_exps,
    grad_exps,
    act,
    grad,
    w_in,
    w_out,
    wg,
    fwd_code,
    bwd_code,
    entries,
    targets,
    lim_act,
    lim_grad,
    x_back,
    x_now,
    g_all,
    y_send,
    y_recv,
    d_send,
    d_recv,
    u_back,
    r_back,
    a_back,
    du_tick,
    factors,
    x_gather,
    g_gather,
    f_gather,
    p_send,
    p_recv,
    load_sem,
    entry_send,
    entry_recv,
    y_send_sem,
    y_recv_sem,
    d_send_sem,
    d_recv_sem,
    x_send_sem,
    x_recv_sem,
    g_send_sem,
    g_recv_sem,
    f_send_sem,
    f_recv_sem,
    p_send_sem,
    p_recv_sem,
    out_sem,
):
    width = w_in.shape[1]
    ring = replicas // 2
    cut = width // ring
    share = width // replicas
    piece = width // sections
    inv_width = 1.0 / width
    s = lax.axis_index("section")
    p = lax.axis_index("dp")
    px = p // 2
    py = p % 2
    first = s == 0
    last = s == sections - 1
    not_first = s > 0
    not_last = s < sections - 1
    mate = px * 2 + (1 - py)

    barrier = pltpu.get_barrier_semaphore()

    def greet(where):
        pl.semaphore_signal(barrier, inc=1, device_id=where, device_id_type=MESH)

    @pl.when(not_first)
    def _():
        greet({"section": s - 1})

    @pl.when(not_last)
    def _():
        greet({"section": s + 1})

    for k in range(1, ring):
        greet({"dp": lax.rem(px + k, ring) * 2 + py})
    greet({"dp": mate})

    @pl.when(first)
    def _():
        def tell(i, c):
            greet({"section": i})
            return c

        lax.fori_loop(1, sections, tell, 0)

    @pl.when(last)
    def _():
        def tell(i, c):
            greet({"section": i})
            return c

        lax.fori_loop(0, sections - 1, tell, 0)

    loads = [
        pltpu.make_async_copy(src, dst, load_sem.at[i])
        for i, (src, dst) in enumerate(
            [
                (act_hbm, act),
                (w_in_hbm, w_in),
                (fwd_inflow, fwd_code),
                (w_out_hbm, w_out),
                (grad_hbm, grad),
                (bwd_inflow, bwd_code),
                (act_hbm, x_back),
                (fwd_rows_hbm, fwd_rows),
                (bwd_rows_hbm, bwd_rows),
                (gain_hbm, gain_ref),
                (act_exps_hbm, act_exps),
                (grad_exps_hbm, grad_exps),
            ]
        )
    ]
    for i in (10, 11, 9, 1, 7, 8, 0, 2, 3, 4, 5):
        loads[i].start()

    @pl.when(not_last)
    def _():
        loads[6].start()

    count = (
        jnp.where(not_first, 2, 0) + jnp.where(not_last, 2, 0) + (ring - 1) + 1
    )
    pl.semaphore_wait(barrier, count)

    mine = pl.ds(pl.multiple_of(s * piece, 128), piece)

    def entry_copy(which, t):
        src = (entry_hbm, target_hbm)[which]
        dst = (entries, targets)[which]
        return pltpu.make_async_remote_copy(
            src_ref=src.at[t],
            dst_ref=dst.at[t, :, mine],
            send_sem=entry_send.at[which, t],
            recv_sem=entry_recv.at[which, t],
            device_id={"section": (0, sections - 1)[which]},
            device_id_type=MESH,
        )

    def entry_local(which, t):
        src = (entry_hbm, target_hbm)[which]
        dst = (entries, targets)[which]
        return pltpu.make_async_copy(
            src.at[t], dst.at[t, :, mine], entry_recv.at[which, t]
        )

    def entry_wait(which, t):
        dst = (entries, targets)[which]
        pltpu.make_async_copy(dst.at[t], dst.at[t], entry_recv.at[which, t]).wait()

    for t in range(TICKS):
        for which, away, here in ((0, not_first, first), (1, not_last, last)):

            @pl.when(away)
            def _():
                entry_copy(which, t).start()

            @pl.when(here)
            def _():
                entry_local(which, t).start()

    def columns(j):
        return pl.ds(pl.multiple_of(j * cut, 128), cut)

    def spread(src, dst, send_sem, recv_sem, slot, j):
        @pl.when(j != px)
        def _():
            pltpu.make_async_remote_copy(
                src_ref=src.at[slot, :, columns(j)],
                dst_ref=dst.at[px, slot],
                send_sem=send_sem.at[slot, j],
                recv_sem=recv_sem.at[px, slot],
                device_id={"dp": j * 2 + py},
                device_id_type=MESH,
            ).start()

        @pl.when(j == px)
        def _():
            pltpu.make_async_copy(
                src.at[slot, :, columns(j)], dst.at[px, slot], recv_sem.at[px, slot]
            ).start()

    def spread_wait(src, dst, send_sem, recv_sem):
        def one(i, c):
            k, slot = i // TICKS, i % TICKS

            @pl.when(k != px)
            def _():
                copy = pltpu.make_async_remote_copy(
                    src_ref=src.at[slot, :, columns(k)],
                    dst_ref=dst.at[k, slot],
                    send_sem=send_sem.at[slot, k],
                    recv_sem=recv_sem.at[k, slot],
                    device_id={"dp": k * 2 + py},
                    device_id_type=MESH,
                )
                copy.wait_recv()
                copy.wait_send()

            @pl.when(k == px)
            def _():
                pltpu.make_async_copy(
                    src.at[slot, :, columns(k)], dst.at[k, slot], recv_sem.at[k, slot]
                ).wait()

            return c

        lax.fori_loop(0, ring * TICKS, one, 0)

    def x_spread(slot, j):
        spread(x_back, x_gather, x_send_sem, x_recv_sem, slot, j)

    def g_spread(slot, j):
        spread(g_all, g_gather, g_send_sem, g_recv_sem, slot, j)

    @pl.when(not_last)
    def _():
        loads[6].wait()
        for slot in range(TICKS):
            for k in range(ring):
                x_spread(slot, lax.rem(px + k, ring))

    blocks = act_exps.shape[-1]

    def expand(exps, rows, limits, t):
        scale = jnp.exp2(exps[rows[0, t]].astype(F32) + 4.0)
        for j in range(ring):
            limits[t, :, j * cut : (j + 1) * cut] = jnp.concatenate(
                [
                    jnp.broadcast_to(scale[:, b : b + 1], (ROWS, 128))
                    for b in range(j * blocks // ring, (j + 1) * blocks // ring)
                ],
                axis=1,
            ).astype(BF16)

    def expand_forward(t):
        expand(act_exps, fwd_rows, lim_act, t)

    def expand_backward(t):
        expand(grad_exps, bwd_rows, lim_grad, t)

    loads[1].wait()
    loads[9].wait()

    def fold(j, c):
        wg[:, columns(j)] = (
            w_in[:, columns(j)].astype(F32) * gain_ref[:, columns(j)].astype(F32)
        ).astype(BF16)
        return c

    lax.fori_loop(0, ring, fold, 0)
    loads[0].wait()
    loads[2].wait()
    loads[3].wait()
    loads[7].wait()
    loads[8].wait()
    loads[10].wait()
    loads[11].wait()

    def y_copy(t, j):
        return pltpu.make_async_remote_copy(
            src_ref=y_send.at[t, :, columns(j)],
            dst_ref=y_recv.at[t, :, columns(j)],
            send_sem=y_send_sem.at[t, j],
            recv_sem=y_recv_sem.at[t, j],
            device_id={"section": s + 1},
            device_id_type=MESH,
        )

    def d_copy(t, j):
        return pltpu.make_async_remote_copy(
            src_ref=d_send.at[t, :, columns(j)],
            dst_ref=d_recv.at[t, :, columns(j)],
            send_sem=d_send_sem.at[t, j],
            recv_sem=d_recv_sem.at[t, j],
            device_id={"section": s - 1},
            device_id_type=MESH,
        )

    def scaled(cache, limit, code):
        return (
            cache.astype(F32) + limit.astype(F32) * 0.0625 * code.astype(F32)
        ).astype(BF16)

    def clipped(cache, limit, value):
        cache, limit, value = cache.astype(F32), limit.astype(F32), value.astype(F32)
        return jnp.minimum(jnp.maximum(value, cache - limit), cache + limit).astype(BF16)

    def forward(t):
        row = fwd_rows[0, t]

        @pl.when(first)
        def _():
            entry_wait(0, t)

        def take(j, c):
            total, u = c
            at = columns(j)
            cache, limit = act[row, :, at], lim_act[t, :, at]
            if t == 0:

                @pl.when(first)
                def _():
                    x_now[:, at] = scaled(cache, limit, entries[t, :, at])

                @pl.when(not_first)
                def _():
                    x_now[:, at] = scaled(cache, limit, fwd_code[:, at])

            else:

                @pl.when(first)
                def _():
                    x_now[:, at] = scaled(cache, limit, entries[t, :, at])

                @pl.when(not_first)
                def _():
                    y_copy(t - 1, j).wait_recv()
                    x_now[:, at] = clipped(cache, limit, y_recv[t - 1, :, at])

            x = x_now[:, at]
            xf = x.astype(F32)
            total = total + jnp.sum(xf * xf, axis=1, keepdims=True)
            u = u + dot_last(x, wg[:, at])

            @pl.when(last)
            def _():
                x_back[t, :, at] = x
                x_spread(t, j)

            return total, u

        total, u = lax.fori_loop(
            0,
            ring,
            take,
            (jnp.zeros((ROWS, 1), F32), jnp.zeros((ROWS, w_in.shape[0]), F32)),
        )
        r = lax.rsqrt(total * inv_width + 1e-05)
        u = u * r
        a = gelu(u).astype(BF16)

        @pl.when(last)
        def _():
            u_back[t] = u
            r_back[t] = jnp.broadcast_to(r, (ROWS, 128))
            a_back[t] = a
            entry_wait(1, t)

        def give(j, c):
            at = columns(j)
            y = x_now[:, at].astype(F32) + dot_plain(a, w_out[:, at])
            y_send[t, :, at] = y.astype(BF16)
            if t < TICKS - 1:

                @pl.when(not_last)
                def _():
                    y_copy(t, j).start()

            @pl.when(last)
            def _():
                g_all[t, :, at] = (y - targets[t, :, at].astype(F32)).astype(BF16)

            return c

        lax.fori_loop(0, ring, give, 0)
        if t == TICKS - 1:
            pltpu.make_async_copy(y_send.at[t], fwd_out, out_sem.at[0]).start()

    def prepare_backward():
        def take(j, c):
            total, u = c
            at = columns(j)
            x = x_back[:, :, at].reshape(TICKS * ROWS, cut)
            xf = x.astype(F32)
            return (
                total + jnp.sum(xf * xf, axis=1, keepdims=True),
                u + dot_last(x, wg[:, at]),
            )

        total, u = lax.fori_loop(
            0,
            ring,
            take,
            (
                jnp.zeros((TICKS * ROWS, 1), F32),
                jnp.zeros((TICKS * ROWS, w_in.shape[0]), F32),
            ),
        )
        r = lax.rsqrt(total * inv_width + 1e-05)
        u = u * r
        u_back[...] = u.reshape(u_back.shape)
        r_back[...] = jnp.broadcast_to(r, (TICKS * ROWS, 128)).reshape(r_back.shape)
        a_back[...] = gelu(u).astype(BF16).reshape(a_back.shape)

    def backward_take(t):
        row = bwd_rows[0, t]
        used = jnp.where(last, t, row)

        def take(j, c):
            at = columns(j)

            @pl.when(not_last)
            def _():
                cache, limit = grad[row, :, at], lim_grad[t, :, at]
                if t == 0:
                    g_all[t, :, at] = scaled(cache, limit, bwd_code[:, at])
                else:
                    d_copy(t - 1, j).wait_recv()
                    g_all[t, :, at] = clipped(cache, limit, d_recv[t - 1, :, at])

            g_spread(t, j)
            return c + dot_last(g_all[t, :, at], w_out[:, at])

        d_active = lax.fori_loop(
            0, ring, take, jnp.zeros((ROWS, w_in.shape[0]), F32)
        )
        u = u_back[used]
        r = r_back[used][:, :1]
        du = d_active * gelu_slope(u)
        shift = r * r * (jnp.sum(du * u, axis=1, keepdims=True) * inv_width)
        du_tick[t] = (du * r).astype(BF16)
        factors[1, t] = a_back[used]
        return used, r, shift, du.astype(BF16)

    def backward_give(t, held):
        used, r, shift, du = held

        def give(j, c):
            at = columns(j)
            dx = (
                g_all[t, :, at].astype(F32)
                + r * dot_plain(du, wg[:, at])
                - x_back[used, :, at].astype(F32) * shift
            )
            d_send[t, :, at] = dx.astype(BF16)
            if t < TICKS - 1:

                @pl.when(not_first)
                def _():
                    d_copy(t, j).start()

            return c

        lax.fori_loop(0, ring, give, 0)
        if t == TICKS - 1:
            pltpu.make_async_copy(d_send.at[t], bwd_out, out_sem.at[1]).start()

    def factor_copy(to, frm):
        return pltpu.make_async_remote_copy(
            src_ref=factors,
            dst_ref=f_gather.at[frm],
            send_sem=f_send_sem.at[to],
            recv_sem=f_recv_sem.at[frm],
            device_id={"dp": to * 2 + py},
            device_id_type=MESH,
        )

    def backward(t):
        backward_give(t, backward_take(t))

    def send_factors():
        used = [jnp.where(last, t, bwd_rows[0, t]) for t in range(TICKS)]
        for q in range(TICKS):
            at = 0
            for t in range(1, TICKS):
                at = jnp.where(used[t] == q, t, at)
            factors[0, q] = du_tick[at]
        for k in range(1, ring):
            factor_copy(lax.rem(px + k, ring), px).start()
        pltpu.make_async_copy(factors, f_gather.at[px], f_recv_sem.at[px]).start()

    rows = ring * TICKS * ROWS
    win = w_in.shape[0]

    def product(which, half):
        at = pl.ds(pl.multiple_of(half * share, 128), share)
        data = (x_gather, g_gather)[which]
        return dot_first(
            f_gather[:, which].reshape(rows, win),
            data[:, :, :, at].reshape(rows, share),
        )

    def swap(which):
        return pltpu.make_async_remote_copy(
            src_ref=p_send.at[which],
            dst_ref=p_recv.at[which],
            send_sem=p_send_sem.at[which],
            recv_sem=p_recv_sem.at[which],
            device_id={"dp": mate},
            device_id_type=MESH,
        )

    def give_product(which):
        p_send[which] = product(which, 1 - py).astype(BF16)
        swap(which).start()

    def first_products():
        pltpu.make_async_copy(factors, f_gather.at[px], f_recv_sem.at[px]).wait()
        for k in range(1, ring):
            other = lax.rem(px + k, ring)
            factor_copy(other, other).wait()
        spread_wait(x_back, x_gather, x_send_sem, x_recv_sem)
        give_product(0)

    def second_products():
        spread_wait(g_all, g_gather, g_send_sem, g_recv_sem)
        give_product(1)

    def rest_of_limits():
        def one(t, c):
            expand_forward(t)
            expand_backward(t)
            return c

        lax.fori_loop(1, TICKS, one, 0)

    def ready_backward():
        @pl.when(not_last)
        def _():
            prepare_backward()

        expand_backward(0)
        loads[4].wait()
        loads[5].wait()

    @pl.when(s % 2 == 1)
    def _():
        expand_forward(0)
        forward(0)
        ready_backward()
        backward(0)
        rest_of_limits()
        for t in range(1, TICKS - 1):
            forward(t)
            backward(t)
        forward(TICKS - 1)
        held = backward_take(TICKS - 1)
        send_factors()
        backward_give(TICKS - 1, held)
        first_products()
        second_products()

    @pl.when(s % 2 == 0)
    def _():
        ready_backward()
        backward(0)
        expand_forward(0)
        forward(0)
        rest_of_limits()
        for t in range(1, TICKS - 1):
            backward(t)
            forward(t)
        held = backward_take(TICKS - 1)
        send_factors()
        backward_give(TICKS - 1, held)
        first_products()
        forward(TICKS - 1)
        second_products()

    factor = 1.0 / (TICKS * replicas)
    at = pl.ds(pl.multiple_of(p * share, 128), share)
    own = product(0, py)
    swap(0).wait()
    total = own + p_recv[0].astype(F32)
    gw_in_out[...] = (total * (gain_ref[:, at].astype(F32) * factor)).astype(BF16)
    ggain_out[...] = (
        jnp.sum(total * w_in[:, at].astype(F32), axis=0, keepdims=True) * factor
    )
    own = product(1, py)
    swap(1).wait()
    gw_out_out[...] = ((own + p_recv[1].astype(F32)) * factor).astype(BF16)

    for t in range(TICKS):

        @pl.when(not_first)
        def _():
            entry_copy(0, t).wait_send()

        @pl.when(not_last)
        def _():
            entry_copy(1, t).wait_send()

    for t in range(TICKS - 1):
        for j in range(ring):

            @pl.when(not_last)
            def _():
                y_copy(t, j).wait_send()

            @pl.when(not_first)
            def _():
                d_copy(t, j).wait_send()

    pltpu.make_async_copy(y_send.at[TICKS - 1], fwd_out, out_sem.at[0]).wait()
    pltpu.make_async_copy(d_send.at[TICKS - 1], bwd_out, out_sem.at[1]).wait()


def hand_over(*refs):
    sources, results, held, sem = refs[:5], refs[5:10], refs[10:15], refs[15]
    takes = [
        pltpu.make_async_copy(src, mid, sem.at[0, i])
        for i, (src, mid) in enumerate(zip(sources, held))
    ]
    gives = [
        pltpu.make_async_copy(mid, dst, sem.at[1, i])
        for i, (mid, dst) in enumerate(zip(held, results))
    ]
    for take in takes:
        take.start()
    for take, give in zip(takes, gives):
        take.wait()
        give.start()
    for give in gives:
        give.wait()


def solution(mesh):
    sections = mesh.shape["section"]
    replicas = mesh.shape["dp"]

    def body(
        entry_codes,
        loss_target,
        fwd_inflow,
        bwd_inflow,
        act_cache,
        act_exps,
        grad_cache,
        grad_exps,
        fwd_rows,
        bwd_rows,
        norm_gain,
        w_in,
        w_out,
    ):
        win, width = w_in.shape[1:]
        ring = replicas // 2
        cut = width // ring
        share = width // replicas
        blocks = act_exps.shape[-1]
        full = (ROWS, width)
        dma = pltpu.SemaphoreType.DMA
        hbm = pl.BlockSpec(memory_space=pltpu.HBM)
        vmem = pl.BlockSpec(memory_space=pltpu.VMEM)
        outs = pl.pallas_call(
            functools.partial(kernel, sections, replicas),
            out_shape=(
                jax.ShapeDtypeStruct((win, share), BF16),
                jax.ShapeDtypeStruct((win, share), BF16),
                jax.ShapeDtypeStruct((1, share), F32),
                jax.ShapeDtypeStruct(full, BF16),
                jax.ShapeDtypeStruct(full, BF16),
            ),
            in_specs=[hbm] * 13,
            out_specs=(vmem, vmem, vmem, hbm, hbm),
            scratch_shapes=[
                pltpu.SMEM((1, TICKS), jnp.int32),
                pltpu.SMEM((1, TICKS), jnp.int32),
                pltpu.VMEM((1, width), BF16),
                pltpu.VMEM((TICKS, ROWS, blocks), jnp.int32),
                pltpu.VMEM((TICKS, ROWS, blocks), jnp.int32),
                pltpu.VMEM((TICKS,) + full, BF16),
                pltpu.VMEM((TICKS,) + full, BF16),
                pltpu.VMEM((win, width), BF16),
                pltpu.VMEM((win, width), BF16),
                pltpu.VMEM((win, width), BF16),
                pltpu.VMEM(full, BF16),
                pltpu.VMEM(full, BF16),
                pltpu.VMEM((TICKS,) + full, BF16),
                pltpu.VMEM((TICKS,) + full, BF16),
                pltpu.VMEM((TICKS,) + full, BF16),
                pltpu.VMEM((TICKS,) + full, BF16),
                pltpu.VMEM((TICKS,) + full, BF16),
                pltpu.VMEM(full, BF16),
                pltpu.VMEM((TICKS,) + full, BF16),
                pltpu.VMEM((TICKS,) + full, BF16),
                pltpu.VMEM((TICKS - 1,) + full, BF16),
                pltpu.VMEM((TICKS,) + full, BF16),
                pltpu.VMEM((TICKS - 1,) + full, BF16),
                pltpu.VMEM((TICKS, ROWS, win), F32),
                pltpu.VMEM((TICKS, ROWS, 128), F32),
                pltpu.VMEM((TICKS, ROWS, win), BF16),
                pltpu.VMEM((TICKS, ROWS, win), BF16),
                pltpu.VMEM((2, TICKS, ROWS, win), BF16),
                pltpu.VMEM((ring, TICKS, ROWS, cut), BF16),
                pltpu.VMEM((ring, TICKS, ROWS, cut), BF16),
                pltpu.VMEM((ring, 2, TICKS, ROWS, win), BF16),
                pltpu.VMEM((2, win, share), BF16),
                pltpu.VMEM((2, win, share), BF16),
                dma((12,)),
                dma((2, TICKS)),
                dma((2, TICKS)),
                dma((TICKS - 1, ring)),
                dma((TICKS - 1, ring)),
                dma((TICKS - 1, ring)),
                dma((TICKS - 1, ring)),
                dma((TICKS, ring)),
                dma((ring, TICKS)),
                dma((TICKS, ring)),
                dma((ring, TICKS)),
                dma((ring,)),
                dma((ring,)),
                dma((2,)),
                dma((2,)),
                dma((2,)),
            ],
            compiler_params=pltpu.CompilerParams(
                collective_id=0,
                has_side_effects=True,
                vmem_limit_bytes=VMEM_BYTES,
            ),
        )(
            fwd_rows,
            bwd_rows,
            norm_gain,
            act_exps[0],
            grad_exps[0],
            entry_codes,
            loss_target,
            fwd_inflow[0],
            bwd_inflow[0],
            act_cache[0],
            grad_cache[0],
            w_in[0],
            w_out[0],
        )
        gw_in, gw_out, ggain, fwd_last, bwd_last = pl.pallas_call(
            hand_over,
            out_shape=tuple(jax.ShapeDtypeStruct(o.shape, o.dtype) for o in outs),
            in_specs=[pl.BlockSpec(memory_space=pl.ANY)] * 5,
            out_specs=(hbm,) * 5,
            scratch_shapes=[pltpu.VMEM(o.shape, o.dtype) for o in outs] + [dma((2, 5))],
            compiler_params=pltpu.CompilerParams(vmem_limit_bytes=VMEM_BYTES),
        )(*outs)
        return gw_in[None], gw_out[None], ggain, fwd_last[None], bwd_last[None]

    return jax.shard_map(
        body,
        mesh=mesh,
        in_specs=(
            P(None, "dp", "section"),
            P(None, "dp", "section"),
            P("section", "dp", None),
            P("section", "dp", None),
            P("section", "dp", None, None),
            P("section", "dp", None, None),
            P("section", "dp", None, None),
            P("section", "dp", None, None),
            P("section", "dp"),
            P("section", "dp"),
            P("section", None),
            P("section", None, None),
            P("section", None, None),
        ),
        out_specs=(
            P("section", None, "dp"),
            P("section", None, "dp"),
            P("section", "dp"),
            P("section", "dp", None),
            P("section", "dp", None),
        ),
        check_vma=False,
    )
```

```python
import functools

import jax
import jax.numpy as jnp
from jax import lax
from jax.experimental import pallas as pl
from jax.experimental.pallas import tpu as pltpu
from jax.sharding import PartitionSpec as P

MESH = pl.DeviceIdType.MESH
ROWS = 16
TICKS = 4
VMEM_BYTES = 64 * 1024 * 1024
F32 = jnp.float32
BF16 = jnp.bfloat16


def dot_last(a, b):
    return lax.dot_general(a, b, (((1,), (1,)), ((), ())), preferred_element_type=F32)


def dot_first(a, b):
    return lax.dot_general(a, b, (((0,), (0,)), ((), ())), preferred_element_type=F32)


def dot_plain(a, b):
    return lax.dot_general(a, b, (((1,), (0,)), ((), ())), preferred_element_type=F32)


def half_erf(u):
    return 0.5 * (1.0 + lax.erf(u * 0.7071067811865476))


def gelu(u):
    return u * half_erf(u)


def gelu_slope(u):
    return half_erf(u) + u * jnp.exp(-0.5 * u * u) * 0.3989422804014327


def kernel(
    sections,
    replicas,
    fwd_rows_hbm,
    bwd_rows_hbm,
    gain_hbm,
    act_exps_hbm,
    grad_exps_hbm,
    entry_hbm,
    target_hbm,
    fwd_inflow,
    bwd_inflow,
    act_hbm,
    grad_hbm,
    w_in_hbm,
    w_out_hbm,
    gw_in_out,
    gw_out_out,
    ggain_out,
    fwd_out,
    bwd_out,
    fwd_rows,
    bwd_rows,
    gain_ref,
    act_exps,
    grad_exps,
    act,
    grad,
    w_in,
    w_out,
    wg,
    fwd_code,
    bwd_code,
    entries,
    targets,
    lim_act,
    lim_grad,
    x_back,
    x_now,
    g_all,
    y_send,
    y_recv,
    d_send,
    d_recv,
    u_back,
    r_back,
    a_back,
    du_tick,
    factors,
    x_gather,
    g_gather,
    f_gather,
    p_send,
    p_recv,
    load_sem,
    entry_send,
    entry_recv,
    y_send_sem,
    y_recv_sem,
    d_send_sem,
    d_recv_sem,
    x_send_sem,
    x_recv_sem,
    g_send_sem,
    g_recv_sem,
    f_send_sem,
    f_recv_sem,
    p_send_sem,
    p_recv_sem,
    out_sem,
):
    width = w_in.shape[1]
    ring = replicas // 2
    cut = width // ring
    share = width // replicas
    piece = width // sections
    inv_width = 1.0 / width
    s = lax.axis_index("section")
    p = lax.axis_index("dp")
    px = p // 2
    py = p % 2
    first = s == 0
    last = s == sections - 1
    not_first = s > 0
    not_last = s < sections - 1
    mate = px * 2 + (1 - py)

    barrier = pltpu.get_barrier_semaphore()

    def greet(where):
        pl.semaphore_signal(barrier, inc=1, device_id=where, device_id_type=MESH)

    @pl.when(not_first)
    def _():
        greet({"section": s - 1})

    @pl.when(not_last)
    def _():
        greet({"section": s + 1})

    for k in range(1, ring):
        greet({"dp": lax.rem(px + k, ring) * 2 + py})
    greet({"dp": mate})

    @pl.when(first)
    def _():
        def tell(i, c):
            greet({"section": i})
            return c

        lax.fori_loop(1, sections, tell, 0)

    @pl.when(last)
    def _():
        def tell(i, c):
            greet({"section": i})
            return c

        lax.fori_loop(0, sections - 1, tell, 0)

    loads = [
        pltpu.make_async_copy(src, dst, load_sem.at[i])
        for i, (src, dst) in enumerate(
            [
                (act_hbm, act),
                (w_in_hbm, w_in),
                (fwd_inflow, fwd_code),
                (w_out_hbm, w_out),
                (grad_hbm, grad),
                (bwd_inflow, bwd_code),
                (act_hbm, x_back),
                (fwd_rows_hbm, fwd_rows),
                (bwd_rows_hbm, bwd_rows),
                (gain_hbm, gain_ref),
                (act_exps_hbm, act_exps),
                (grad_exps_hbm, grad_exps),
            ]
        )
    ]
    for i in (10, 11, 9, 1, 7, 8, 0, 2, 3, 4, 5):
        loads[i].start()

    @pl.when(not_last)
    def _():
        loads[6].start()

    count = (
        jnp.where(not_first, 2, 0) + jnp.where(not_last, 2, 0) + (ring - 1) + 1
    )
    pl.semaphore_wait(barrier, count)

    mine = pl.ds(pl.multiple_of(s * piece, 128), piece)

    def entry_copy(which, t):
        src = (entry_hbm, target_hbm)[which]
        dst = (entries, targets)[which]
        return pltpu.make_async_remote_copy(
            src_ref=src.at[t],
            dst_ref=dst.at[t, :, mine],
            send_sem=entry_send.at[which, t],
            recv_sem=entry_recv.at[which, t],
            device_id={"section": (0, sections - 1)[which]},
            device_id_type=MESH,
        )

    def entry_local(which, t):
        src = (entry_hbm, target_hbm)[which]
        dst = (entries, targets)[which]
        return pltpu.make_async_copy(
            src.at[t], dst.at[t, :, mine], entry_recv.at[which, t]
        )

    def entry_wait(which, t):
        dst = (entries, targets)[which]
        pltpu.make_async_copy(dst.at[t], dst.at[t], entry_recv.at[which, t]).wait()

    def start_entries(t):
        for which, away, here in ((0, not_first, first), (1, not_last, last)):

            @pl.when(away)
            def _():
                entry_copy(which, t).start()

            @pl.when(here)
            def _():
                entry_local(which, t).start()

    start_entries(0)

    def columns(j):
        return pl.ds(pl.multiple_of(j * cut, 128), cut)

    def half_columns(j, part):
        half = 1 - py if part == 0 else py
        return pl.ds(pl.multiple_of(j * cut + half * share, 128), share)

    def spread(refs, slot, j, part, src=None):
        held, dst, send_sem, recv_sem = refs
        src = held if src is None else src
        index = slot * 2 + part

        @pl.when(j != px)
        def _():
            pltpu.make_async_remote_copy(
                src_ref=src.at[slot, :, half_columns(j, part)],
                dst_ref=dst.at[px, slot, :, half_columns(0, part)],
                send_sem=send_sem.at[index, j],
                recv_sem=recv_sem.at[px, index],
                device_id={"dp": j * 2 + py},
                device_id_type=MESH,
            ).start()

        @pl.when(j == px)
        def _():
            pltpu.make_async_copy(
                src.at[slot, :, half_columns(j, part)],
                dst.at[px, slot, :, half_columns(0, part)],
                recv_sem.at[px, index],
            ).start()

    def spread_all(refs, slot, part, src=None):
        for k in range(ring):
            spread(refs, slot, lax.rem(px + k, ring), part, src)

    def spread_wait(refs, part):
        src, dst, send_sem, recv_sem = refs

        def one(i, c):
            slot, k = i // ring, i % ring
            index = slot * 2 + part

            @pl.when(k != px)
            def _():
                copy = pltpu.make_async_remote_copy(
                    src_ref=src.at[slot, :, half_columns(k, part)],
                    dst_ref=dst.at[k, slot, :, half_columns(0, part)],
                    send_sem=send_sem.at[index, k],
                    recv_sem=recv_sem.at[k, index],
                    device_id={"dp": k * 2 + py},
                    device_id_type=MESH,
                )
                copy.wait_recv()
                copy.wait_send()

            @pl.when(k == px)
            def _():
                pltpu.make_async_copy(
                    src.at[slot, :, half_columns(k, part)],
                    dst.at[k, slot, :, half_columns(0, part)],
                    recv_sem.at[k, index],
                ).wait()

            return c

        lax.fori_loop(0, ring * TICKS, one, 0)

    x_refs = (x_back, x_gather, x_send_sem, x_recv_sem)
    g_refs = (g_all, g_gather, g_send_sem, g_recv_sem)

    @pl.when(not_last)
    def _():
        for slot in range(TICKS):
            spread_all(x_refs, slot, 0, act_hbm)

    for t in range(1, TICKS):
        start_entries(t)

    blocks = act_exps.shape[-1]

    def expand(exps, rows, limits, t):
        scale = jnp.exp2(exps[rows[0, t]].astype(F32) + 4.0)
        for j in range(ring):
            limits[t, :, j * cut : (j + 1) * cut] = jnp.concatenate(
                [
                    jnp.broadcast_to(scale[:, b : b + 1], (ROWS, 128))
                    for b in range(j * blocks // ring, (j + 1) * blocks // ring)
                ],
                axis=1,
            ).astype(BF16)

    def expand_forward(t):
        expand(act_exps, fwd_rows, lim_act, t)

    def expand_backward(t):
        expand(grad_exps, bwd_rows, lim_grad, t)

    loads[1].wait()
    loads[9].wait()

    def fold(j, c):
        wg[:, columns(j)] = (
            w_in[:, columns(j)].astype(F32) * gain_ref[:, columns(j)].astype(F32)
        ).astype(BF16)
        return c

    lax.fori_loop(0, ring, fold, 0)
    loads[0].wait()
    loads[2].wait()
    loads[3].wait()
    loads[7].wait()
    loads[8].wait()
    loads[10].wait()
    loads[11].wait()

    def y_copy(t, j):
        return pltpu.make_async_remote_copy(
            src_ref=y_send.at[t, :, columns(j)],
            dst_ref=y_recv.at[t, :, columns(j)],
            send_sem=y_send_sem.at[t, j],
            recv_sem=y_recv_sem.at[t, j],
            device_id={"section": s + 1},
            device_id_type=MESH,
        )

    def d_copy(t, j):
        return pltpu.make_async_remote_copy(
            src_ref=d_send.at[t, :, columns(j)],
            dst_ref=d_recv.at[t, :, columns(j)],
            send_sem=d_send_sem.at[t, j],
            recv_sem=d_recv_sem.at[t, j],
            device_id={"section": s - 1},
            device_id_type=MESH,
        )

    def scaled(cache, limit, code):
        return (
            cache.astype(F32) + limit.astype(F32) * 0.0625 * code.astype(F32)
        ).astype(BF16)

    def clipped(cache, limit, value):
        cache, limit, value = cache.astype(F32), limit.astype(F32), value.astype(F32)
        return jnp.minimum(jnp.maximum(value, cache - limit), cache + limit).astype(BF16)

    def forward(t):
        row = fwd_rows[0, t]

        @pl.when(first)
        def _():
            entry_wait(0, t)

        def take(j, c):
            total, u = c
            at = columns(j)
            cache, limit = act[row, :, at], lim_act[t, :, at]
            if t == 0:

                @pl.when(first)
                def _():
                    x_now[:, at] = scaled(cache, limit, entries[t, :, at])

                @pl.when(not_first)
                def _():
                    x_now[:, at] = scaled(cache, limit, fwd_code[:, at])

            else:

                @pl.when(first)
                def _():
                    x_now[:, at] = scaled(cache, limit, entries[t, :, at])

                @pl.when(not_first)
                def _():
                    y_copy(t - 1, j).wait_recv()
                    x_now[:, at] = clipped(cache, limit, y_recv[t - 1, :, at])

            x = x_now[:, at]
            xf = x.astype(F32)
            total = total + jnp.sum(xf * xf, axis=1, keepdims=True)
            u = u + dot_last(x, wg[:, at])

            @pl.when(last)
            def _():
                x_back[t, :, at] = x
                spread(x_refs, t, j, 0)
                spread(x_refs, t, j, 1)

            return total, u

        total, u = lax.fori_loop(
            0,
            ring,
            take,
            (jnp.zeros((ROWS, 1), F32), jnp.zeros((ROWS, w_in.shape[0]), F32)),
        )
        r = lax.rsqrt(total * inv_width + 1e-05)
        u = u * r
        a = gelu(u).astype(BF16)

        @pl.when(last)
        def _():
            u_back[t] = u
            r_back[t] = jnp.broadcast_to(r, (ROWS, 128))
            a_back[t] = a
            entry_wait(1, t)

        def give(j, c):
            at = columns(j)
            y = x_now[:, at].astype(F32) + dot_plain(a, w_out[:, at])
            y_send[t, :, at] = y.astype(BF16)
            if t < TICKS - 1:

                @pl.when(not_last)
                def _():
                    y_copy(t, j).start()

            @pl.when(last)
            def _():
                g_all[t, :, at] = (y - targets[t, :, at].astype(F32)).astype(BF16)

            return c

        lax.fori_loop(0, ring, give, 0)
        if t == TICKS - 1:
            pltpu.make_async_copy(y_send.at[t], fwd_out, out_sem.at[0]).start()

    def prepare_backward():
        def take(j, c):
            total, u = c
            at = columns(j)
            x = x_back[:, :, at].reshape(TICKS * ROWS, cut)
            xf = x.astype(F32)
            return (
                total + jnp.sum(xf * xf, axis=1, keepdims=True),
                u + dot_last(x, wg[:, at]),
            )

        total, u = lax.fori_loop(
            0,
            ring,
            take,
            (
                jnp.zeros((TICKS * ROWS, 1), F32),
                jnp.zeros((TICKS * ROWS, w_in.shape[0]), F32),
            ),
        )
        r = lax.rsqrt(total * inv_width + 1e-05)
        u = u * r
        u_back[...] = u.reshape(u_back.shape)
        r_back[...] = jnp.broadcast_to(r, (TICKS * ROWS, 128)).reshape(r_back.shape)
        a_back[...] = gelu(u).astype(BF16).reshape(a_back.shape)

    def spread_later(t):
        spread_all(g_refs, t, 1)

        @pl.when(not_last)
        def _():
            spread_all(x_refs, t, 1, act_hbm)

    def backward_take(t):
        row = bwd_rows[0, t]
        used = jnp.where(last, t, row)

        def take(j, c):
            at = columns(j)

            @pl.when(not_last)
            def _():
                cache, limit = grad[row, :, at], lim_grad[t, :, at]
                if t == 0:
                    g_all[t, :, at] = scaled(cache, limit, bwd_code[:, at])
                else:
                    d_copy(t - 1, j).wait_recv()
                    g_all[t, :, at] = clipped(cache, limit, d_recv[t - 1, :, at])

            if t < TICKS - 1:
                spread(g_refs, t, j, 0)
            return c + dot_last(g_all[t, :, at], w_out[:, at])

        d_active = lax.fori_loop(
            0, ring, take, jnp.zeros((ROWS, w_in.shape[0]), F32)
        )
        if t < TICKS - 1:
            spread_later(t)
        u = u_back[used]
        r = r_back[used][:, :1]
        du = d_active * gelu_slope(u)
        shift = r * r * (jnp.sum(du * u, axis=1, keepdims=True) * inv_width)
        du_tick[t] = (du * r).astype(BF16)
        factors[1, t] = a_back[used]
        return used, r, shift, du.astype(BF16)

    def backward_give(t, held):
        used, r, shift, du = held

        def give(j, c):
            at = columns(j)
            dx = (
                g_all[t, :, at].astype(F32)
                + r * dot_plain(du, wg[:, at])
                - x_back[used, :, at].astype(F32) * shift
            )
            d_send[t, :, at] = dx.astype(BF16)
            if t < TICKS - 1:

                @pl.when(not_first)
                def _():
                    d_copy(t, j).start()

            return c

        lax.fori_loop(0, ring, give, 0)
        if t == TICKS - 1:
            pltpu.make_async_copy(d_send.at[t], bwd_out, out_sem.at[1]).start()

    def factor_copy(to, frm):
        return pltpu.make_async_remote_copy(
            src_ref=factors,
            dst_ref=f_gather.at[frm],
            send_sem=f_send_sem.at[to],
            recv_sem=f_recv_sem.at[frm],
            device_id={"dp": to * 2 + py},
            device_id_type=MESH,
        )

    def backward(t):
        backward_give(t, backward_take(t))

    def send_factors():
        used = [jnp.where(last, t, bwd_rows[0, t]) for t in range(TICKS)]
        for q in range(TICKS):
            at = 0
            for t in range(1, TICKS):
                at = jnp.where(used[t] == q, t, at)
            factors[0, q] = du_tick[at]
        for k in range(1, ring):
            factor_copy(lax.rem(px + k, ring), px).start()
        pltpu.make_async_copy(factors, f_gather.at[px], f_recv_sem.at[px]).start()

    rows = ring * TICKS * ROWS
    win = w_in.shape[0]

    def product(which, half):
        at = pl.ds(pl.multiple_of(half * share, 128), share)
        data = (x_gather, g_gather)[which]
        return dot_first(
            f_gather[:, which].reshape(rows, win),
            data[:, :, :, at].reshape(rows, share),
        )

    def swap(which):
        return pltpu.make_async_remote_copy(
            src_ref=p_send.at[which],
            dst_ref=p_recv.at[which],
            send_sem=p_send_sem.at[which],
            recv_sem=p_recv_sem.at[which],
            device_id={"dp": mate},
            device_id_type=MESH,
        )

    def give_product(which):
        p_send[which] = product(which, 1 - py).astype(BF16)
        swap(which).start()

    def spread_last_gradient():
        spread_all(g_refs, TICKS - 1, 0)
        spread_later(TICKS - 1)

    def first_products():
        pltpu.make_async_copy(factors, f_gather.at[px], f_recv_sem.at[px]).wait()
        for k in range(1, ring):
            other = lax.rem(px + k, ring)
            factor_copy(other, other).wait()
        spread_wait(x_refs, 0)
        give_product(0)

    def second_products():
        spread_wait(g_refs, 0)
        give_product(1)

    def rest_of_limits():
        def one(t, c):
            expand_forward(t)
            expand_backward(t)
            return c

        lax.fori_loop(1, TICKS, one, 0)

    def ready_backward():
        @pl.when(not_last)
        def _():
            loads[6].wait()
            prepare_backward()

        expand_backward(0)
        loads[4].wait()
        loads[5].wait()

    @pl.when(s % 2 == 1)
    def _():
        expand_forward(0)
        forward(0)
        ready_backward()
        backward(0)
        rest_of_limits()
        for t in range(1, TICKS - 2):
            forward(t)
            backward(t)

        @pl.when(last)
        def _():
            forward(TICKS - 2)

        backward(TICKS - 2)

        @pl.when(not_last)
        def _():
            forward(TICKS - 2)

        forward(TICKS - 1)
        held = backward_take(TICKS - 1)
        send_factors()
        spread_last_gradient()
        backward_give(TICKS - 1, held)
        first_products()
        second_products()

    @pl.when(s % 2 == 0)
    def _():
        ready_backward()
        backward(0)
        expand_forward(0)
        forward(0)
        rest_of_limits()
        for t in range(1, TICKS - 1):
            backward(t)
            forward(t)
        held = backward_take(TICKS - 1)
        send_factors()
        spread_last_gradient()
        backward_give(TICKS - 1, held)
        first_products()
        second_products()
        forward(TICKS - 1)

    factor = 1.0 / (TICKS * replicas)
    at = pl.ds(pl.multiple_of(p * share, 128), share)
    spread_wait(x_refs, 1)
    own = product(0, py)
    swap(0).wait()
    total = own + p_recv[0].astype(F32)
    gw_in_out[...] = (total * (gain_ref[:, at].astype(F32) * factor)).astype(BF16)
    ggain_out[...] = (
        jnp.sum(total * w_in[:, at].astype(F32), axis=0, keepdims=True) * factor
    )
    spread_wait(g_refs, 1)
    own = product(1, py)
    swap(1).wait()
    gw_out_out[...] = ((own + p_recv[1].astype(F32)) * factor).astype(BF16)

    for t in range(TICKS):

        @pl.when(not_first)
        def _():
            entry_copy(0, t).wait_send()

        @pl.when(not_last)
        def _():
            entry_copy(1, t).wait_send()

    for t in range(TICKS - 1):
        for j in range(ring):

            @pl.when(not_last)
            def _():
                y_copy(t, j).wait_send()

            @pl.when(not_first)
            def _():
                d_copy(t, j).wait_send()

    pltpu.make_async_copy(y_send.at[TICKS - 1], fwd_out, out_sem.at[0]).wait()
    pltpu.make_async_copy(d_send.at[TICKS - 1], bwd_out, out_sem.at[1]).wait()


def hand_over(*refs):
    sources, results, held, sem = refs[:5], refs[5:10], refs[10:15], refs[15]
    takes = [
        pltpu.make_async_copy(src, mid, sem.at[0, i])
        for i, (src, mid) in enumerate(zip(sources, held))
    ]
    gives = [
        pltpu.make_async_copy(mid, dst, sem.at[1, i])
        for i, (mid, dst) in enumerate(zip(held, results))
    ]
    for take in takes:
        take.start()
    for take, give in zip(takes, gives):
        take.wait()
        give.start()
    for give in gives:
        give.wait()


def solution(mesh):
    sections = mesh.shape["section"]
    replicas = mesh.shape["dp"]

    def body(
        entry_codes,
        loss_target,
        fwd_inflow,
        bwd_inflow,
        act_cache,
        act_exps,
        grad_cache,
        grad_exps,
        fwd_rows,
        bwd_rows,
        norm_gain,
        w_in,
        w_out,
    ):
        win, width = w_in.shape[1:]
        ring = replicas // 2
        cut = width // ring
        share = width // replicas
        blocks = act_exps.shape[-1]
        full = (ROWS, width)
        dma = pltpu.SemaphoreType.DMA
        hbm = pl.BlockSpec(memory_space=pltpu.HBM)
        vmem = pl.BlockSpec(memory_space=pltpu.VMEM)
        outs = pl.pallas_call(
            functools.partial(kernel, sections, replicas),
            out_shape=(
                jax.ShapeDtypeStruct((win, share), BF16),
                jax.ShapeDtypeStruct((win, share), BF16),
                jax.ShapeDtypeStruct((1, share), F32),
                jax.ShapeDtypeStruct(full, BF16),
                jax.ShapeDtypeStruct(full, BF16),
            ),
            in_specs=[hbm] * 13,
            out_specs=(vmem, vmem, vmem, hbm, hbm),
            scratch_shapes=[
                pltpu.SMEM((1, TICKS), jnp.int32),
                pltpu.SMEM((1, TICKS), jnp.int32),
                pltpu.VMEM((1, width), BF16),
                pltpu.VMEM((TICKS, ROWS, blocks), jnp.int32),
                pltpu.VMEM((TICKS, ROWS, blocks), jnp.int32),
                pltpu.VMEM((TICKS,) + full, BF16),
                pltpu.VMEM((TICKS,) + full, BF16),
                pltpu.VMEM((win, width), BF16),
                pltpu.VMEM((win, width), BF16),
                pltpu.VMEM((win, width), BF16),
                pltpu.VMEM(full, BF16),
                pltpu.VMEM(full, BF16),
                pltpu.VMEM((TICKS,) + full, BF16),
                pltpu.VMEM((TICKS,) + full, BF16),
                pltpu.VMEM((TICKS,) + full, BF16),
                pltpu.VMEM((TICKS,) + full, BF16),
                pltpu.VMEM((TICKS,) + full, BF16),
                pltpu.VMEM(full, BF16),
                pltpu.VMEM((TICKS,) + full, BF16),
                pltpu.VMEM((TICKS,) + full, BF16),
                pltpu.VMEM((TICKS - 1,) + full, BF16),
                pltpu.VMEM((TICKS,) + full, BF16),
                pltpu.VMEM((TICKS - 1,) + full, BF16),
                pltpu.VMEM((TICKS, ROWS, win), F32),
                pltpu.VMEM((TICKS, ROWS, 128), F32),
                pltpu.VMEM((TICKS, ROWS, win), BF16),
                pltpu.VMEM((TICKS, ROWS, win), BF16),
                pltpu.VMEM((2, TICKS, ROWS, win), BF16),
                pltpu.VMEM((ring, TICKS, ROWS, cut), BF16),
                pltpu.VMEM((ring, TICKS, ROWS, cut), BF16),
                pltpu.VMEM((ring, 2, TICKS, ROWS, win), BF16),
                pltpu.VMEM((2, win, share), BF16),
                pltpu.VMEM((2, win, share), BF16),
                dma((12,)),
                dma((2, TICKS)),
                dma((2, TICKS)),
                dma((TICKS - 1, ring)),
                dma((TICKS - 1, ring)),
                dma((TICKS - 1, ring)),
                dma((TICKS - 1, ring)),
                dma((2 * TICKS, ring)),
                dma((ring, 2 * TICKS)),
                dma((2 * TICKS, ring)),
                dma((ring, 2 * TICKS)),
                dma((ring,)),
                dma((ring,)),
                dma((2,)),
                dma((2,)),
                dma((2,)),
            ],
            compiler_params=pltpu.CompilerParams(
                collective_id=0,
                has_side_effects=True,
                vmem_limit_bytes=VMEM_BYTES,
            ),
        )(
            fwd_rows,
            bwd_rows,
            norm_gain,
            act_exps[0],
            grad_exps[0],
            entry_codes,
            loss_target,
            fwd_inflow[0],
            bwd_inflow[0],
            act_cache[0],
            grad_cache[0],
            w_in[0],
            w_out[0],
        )
        gw_in, gw_out, ggain, fwd_last, bwd_last = pl.pallas_call(
            hand_over,
            out_shape=tuple(jax.ShapeDtypeStruct(o.shape, o.dtype) for o in outs),
            in_specs=[pl.BlockSpec(memory_space=pl.ANY)] * 5,
            out_specs=(hbm,) * 5,
            scratch_shapes=[pltpu.VMEM(o.shape, o.dtype) for o in outs] + [dma((2, 5))],
            compiler_params=pltpu.CompilerParams(vmem_limit_bytes=VMEM_BYTES),
        )(*outs)
        return gw_in[None], gw_out[None], ggain, fwd_last[None], bwd_last[None]

    return jax.shard_map(
        body,
        mesh=mesh,
        in_specs=(
            P(None, "dp", "section"),
            P(None, "dp", "section"),
            P("section", "dp", None),
            P("section", "dp", None),
            P("section", "dp", None, None),
            P("section", "dp", None, None),
            P("section", "dp", None, None),
            P("section", "dp", None, None),
            P("section", "dp"),
            P("section", "dp"),
            P("section", None),
            P("section", None, None),
            P("section", None, None),
        ),
        out_specs=(
            P("section", None, "dp"),
            P("section", None, "dp"),
            P("section", "dp"),
            P("section", "dp", None),
            P("section", "dp", None),
        ),
        check_vma=False,
    )
```

```python
import functools

import jax
import jax.numpy as jnp
from jax import lax
from jax.experimental import pallas as pl
from jax.experimental.pallas import tpu as pltpu
from jax.sharding import PartitionSpec as P

MESH = pl.DeviceIdType.MESH
ROWS = 16
TICKS = 4
VMEM_BYTES = 64 * 1024 * 1024
OPEN = 3e38
F32 = jnp.float32
BF16 = jnp.bfloat16


def dot_last(a, b):
    return lax.dot_general(a, b, (((1,), (1,)), ((), ())), preferred_element_type=F32)


def dot_first(a, b):
    return lax.dot_general(a, b, (((0,), (0,)), ((), ())), preferred_element_type=F32)


def dot_plain(a, b):
    return lax.dot_general(a, b, (((1,), (0,)), ((), ())), preferred_element_type=F32)


def lane_sums(x):
    x = x.astype(F32)
    x = x * x
    return sum(x[:, i : i + 128] for i in range(0, x.shape[1], 128))


def half_erf(u):
    return 0.5 * (1.0 + lax.erf(u * 0.7071067811865476))


def gelu(u):
    return u * half_erf(u)


def gelu_slope(u):
    return half_erf(u) + u * jnp.exp(-0.5 * u * u) * 0.3989422804014327


def kernel(
    sections,
    replicas,
    fwd_rows_hbm,
    bwd_rows_hbm,
    gain_hbm,
    act_exps_hbm,
    grad_exps_hbm,
    entry_hbm,
    target_hbm,
    fwd_inflow,
    bwd_inflow,
    act_hbm,
    grad_hbm,
    w_in_hbm,
    w_out_hbm,
    gw_in_out,
    gw_out_out,
    ggain_out,
    fwd_out,
    bwd_out,
    fwd_rows,
    bwd_rows,
    gain_ref,
    act_exps,
    grad_exps,
    inputs,
    grad,
    w_in,
    w_out,
    wg,
    fwd_code,
    bwd_code,
    entries,
    targets,
    lim_act,
    lim_grad,
    x_now,
    g_all,
    y_send,
    y_recv,
    d_send,
    d_recv,
    u_back,
    slope_back,
    r_back,
    a_back,
    du_tick,
    factors,
    x_gather,
    g_gather,
    f_gather,
    p_send,
    p_recv,
    load_sem,
    mail,
    mail_sem,
    entry_send,
    entry_recv,
    y_send_sem,
    y_recv_sem,
    d_send_sem,
    d_recv_sem,
    x_send_sem,
    x_recv_sem,
    g_send_sem,
    g_recv_sem,
    f_send_sem,
    f_recv_sem,
    p_send_sem,
    p_recv_sem,
    out_sem,
):
    width = w_in.shape[1]
    ring = replicas // 2
    cut = width // ring
    share = width // replicas
    piece = width // sections
    inv_width = 1.0 / width
    act = inputs.at[0]
    s = lax.axis_index("section")
    p = lax.axis_index("dp")
    px = p // 2
    py = p % 2
    first = s == 0
    last = s == sections - 1
    x_from = jnp.where(last, 1, 0)
    not_first = s > 0
    not_last = s < sections - 1
    mate = px * 2 + (1 - py)
    side = s // 2 % 2
    partner = s + 2 - 4 * side

    barrier = pltpu.get_barrier_semaphore()

    def greet(where):
        pl.semaphore_signal(barrier, inc=1, device_id=where, device_id_type=MESH)

    @pl.when(not_first)
    def _():
        greet({"section": s - 1})

    @pl.when(not_last)
    def _():
        greet({"section": s + 1})

    for k in range(1, ring):
        greet({"dp": lax.rem(px + k, ring) * 2 + py})
    greet({"dp": mate})
    greet({"section": partner})

    @pl.when(first)
    def _():
        def tell(i, c):
            greet({"section": i})
            return c

        lax.fori_loop(1, sections, tell, 0)

    @pl.when(last)
    def _():
        def tell(i, c):
            greet({"section": i})
            return c

        lax.fori_loop(0, sections - 1, tell, 0)

    loads = [
        pltpu.make_async_copy(src, dst, load_sem.at[i])
        for i, (src, dst) in enumerate(
            [
                (act_hbm, act),
                (w_in_hbm, w_in),
                (fwd_inflow, fwd_code),
                (w_out_hbm, w_out),
                (grad_hbm, grad),
                (bwd_inflow, bwd_code),
                (fwd_rows_hbm, fwd_rows),
                (bwd_rows_hbm, bwd_rows),
                (gain_hbm, gain_ref),
                (act_exps_hbm, act_exps),
                (grad_exps_hbm, grad_exps),
            ]
        )
    ]
    for i in (9, 10, 8, 6, 7, 1, 0):
        loads[i].start()

    @pl.when(s % 2 == 1)
    def _():
        for i in (2, 3, 4, 5):
            loads[i].start()

    @pl.when(s % 2 == 0)
    def _():
        for i in (4, 5, 3, 2):
            loads[i].start()

    count = (
        jnp.where(not_first, 2, 0) + jnp.where(not_last, 2, 0) + (ring - 1) + 2
    )
    pl.semaphore_wait(barrier, count)

    def mine(owner):
        return pl.ds(pl.multiple_of(owner * piece, 128), piece)

    def mail_copy(src, part):
        at = (pl.ds(0, 1), pl.ds(1, TICKS - 1))[part]
        return pltpu.make_async_remote_copy(
            src_ref=src.at[at],
            dst_ref=mail.at[at],
            send_sem=mail_sem.at[0, part],
            recv_sem=mail_sem.at[1, part],
            device_id={"section": partner},
            device_id_type=MESH,
        )

    def entry_copy(which, t, from_mail):
        src = mail if from_mail else (entry_hbm, target_hbm)[which]
        dst = (entries, targets)[which]
        return pltpu.make_async_remote_copy(
            src_ref=src.at[t],
            dst_ref=dst.at[t, :, mine(partner if from_mail else s)],
            send_sem=entry_send.at[from_mail, t],
            recv_sem=entry_recv.at[which, t],
            device_id={"section": (0, sections - 1)[which]},
            device_id_type=MESH,
        )

    def entry_local(which, t, from_mail):
        src = mail if from_mail else (entry_hbm, target_hbm)[which]
        dst = (entries, targets)[which]
        return pltpu.make_async_copy(
            src.at[t],
            dst.at[t, :, mine(partner if from_mail else s)],
            entry_recv.at[which, t],
        )

    def entry_wait(which, t):
        dst = (entries, targets)[which]
        pltpu.make_async_copy(dst.at[t], dst.at[t], entry_recv.at[which, t]).wait()

    ends = ((0, (side == 0) & not_first, first), (1, (side == 1) & not_last, last))

    def start_entries(t, from_mail):
        for which, away, here in ends:

            @pl.when(away)
            def _():
                entry_copy(which, t, from_mail).start()

            @pl.when(here)
            def _():
                entry_local(which, t, from_mail).start()

    @pl.when(side == 0)
    def _():
        for part in range(2):
            mail_copy(target_hbm, part).start()

    @pl.when(side == 1)
    def _():
        for part in range(2):
            mail_copy(entry_hbm, part).start()

    start_entries(0, 0)

    def columns(j):
        return pl.ds(pl.multiple_of(j * cut, 128), cut)

    def half_columns(j, part):
        half = 1 - py if part == 0 else py
        return pl.ds(pl.multiple_of(j * cut + half * share, 128), share)

    def spread(refs, slot, j, part, src=None):
        held, dst, send_sem, recv_sem = refs
        src = held if src is None else src
        index = slot * 2 + part

        @pl.when(j != px)
        def _():
            pltpu.make_async_remote_copy(
                src_ref=src.at[slot, :, half_columns(j, part)],
                dst_ref=dst.at[px, slot, :, half_columns(0, part)],
                send_sem=send_sem.at[index, j],
                recv_sem=recv_sem.at[px, index],
                device_id={"dp": j * 2 + py},
                device_id_type=MESH,
            ).start()

        @pl.when(j == px)
        def _():
            pltpu.make_async_copy(
                src.at[slot, :, half_columns(j, part)],
                dst.at[px, slot, :, half_columns(0, part)],
                recv_sem.at[px, index],
            ).start()

    def spread_all(refs, slot, part, src=None):
        for k in range(ring):
            spread(refs, slot, lax.rem(px + k, ring), part, src)

    def spread_wait(refs, part):
        src, dst, send_sem, recv_sem = refs

        def one(i, c):
            slot, k = i // ring, i % ring
            index = slot * 2 + part

            @pl.when(k != px)
            def _():
                copy = pltpu.make_async_remote_copy(
                    src_ref=src.at[slot, :, half_columns(k, part)],
                    dst_ref=dst.at[k, slot, :, half_columns(0, part)],
                    send_sem=send_sem.at[index, k],
                    recv_sem=recv_sem.at[k, index],
                    device_id={"dp": k * 2 + py},
                    device_id_type=MESH,
                )
                copy.wait_recv()
                copy.wait_send()

            @pl.when(k == px)
            def _():
                pltpu.make_async_copy(
                    src.at[slot, :, half_columns(k, part)],
                    dst.at[k, slot, :, half_columns(0, part)],
                    recv_sem.at[k, index],
                ).wait()

            return c

        lax.fori_loop(0, ring * TICKS, one, 0)

    x_refs = (inputs.at[1], x_gather, x_send_sem, x_recv_sem)
    g_refs = (g_all, g_gather, g_send_sem, g_recv_sem)

    @pl.when(not_last)
    def _():
        for slot in range(TICKS):
            spread_all(x_refs, slot, 0, act_hbm)

    blocks = act_exps.shape[-1]

    def expand(exps, rows, limits, t):
        scale = jnp.exp2(exps[rows[0, t]].astype(F32) + 4.0)
        for j in range(ring):
            limits[t, :, j * cut : (j + 1) * cut] = jnp.concatenate(
                [
                    jnp.broadcast_to(scale[:, b : b + 1], (ROWS, 128))
                    for b in range(j * blocks // ring, (j + 1) * blocks // ring)
                ],
                axis=1,
            ).astype(BF16)

    def expand_forward(t):
        expand(act_exps, fwd_rows, lim_act, t)

    def expand_backward(t):
        expand(grad_exps, bwd_rows, lim_grad, t)

    loads[1].wait()
    loads[8].wait()

    def fold(j, c):
        wg[:, columns(j)] = (
            w_in[:, columns(j)].astype(F32) * gain_ref[:, columns(j)].astype(F32)
        ).astype(BF16)
        return c

    lax.fori_loop(0, ring, fold, 0)
    mail_copy(target_hbm, 0).wait()
    start_entries(0, 1)
    start_entries(1, 0)
    mail_copy(target_hbm, 1).wait()
    start_entries(1, 1)
    for i in (0, 6, 7, 9, 10):
        loads[i].wait()

    def y_copy(t, j):
        return pltpu.make_async_remote_copy(
            src_ref=y_send.at[t, :, columns(j)],
            dst_ref=y_recv.at[t, :, columns(j)],
            send_sem=y_send_sem.at[t, j],
            recv_sem=y_recv_sem.at[t, j],
            device_id={"section": s + 1},
            device_id_type=MESH,
        )

    def d_copy(t, j):
        return pltpu.make_async_remote_copy(
            src_ref=d_send.at[t, :, columns(j)],
            dst_ref=d_recv.at[t, :, columns(j)],
            send_sem=d_send_sem.at[t, j],
            recv_sem=d_recv_sem.at[t, j],
            device_id={"section": s - 1},
            device_id_type=MESH,
        )

    def scaled(cache, limit, code):
        return (
            cache.astype(F32) + limit.astype(F32) * 0.0625 * code.astype(F32)
        ).astype(BF16)

    def clipped(cache, limit, value):
        return jnp.minimum(jnp.maximum(value, cache - limit), cache + limit)

    def forward(t):
        row = fwd_rows[0, t]

        @pl.when(first)
        def _():
            entry_wait(0, t)
            if t > 0:
                y_recv[t - 1] = scaled(act[row], lim_act[t], entries[t])
                lim_act[t] = jnp.full((ROWS, width), OPEN, BF16)

        def take(j, c):
            total, u = c
            at = columns(j)
            cache, limit = act[row, :, at], lim_act[t, :, at]
            if t == 0:

                @pl.when(first)
                def _():
                    x_now[:, at] = scaled(cache, limit, entries[t, :, at])

                @pl.when(not_first)
                def _():
                    x_now[:, at] = scaled(cache, limit, fwd_code[:, at])

                x = x_now[:, at]
            else:

                @pl.when(not_first)
                def _():
                    y_copy(t - 1, j).wait_recv()

                x = clipped(cache, limit, y_recv[t - 1, :, at])
                x_now[:, at] = x

            total = total + lane_sums(x)
            u = u + dot_last(x, wg[:, at])

            @pl.when(last)
            def _():
                inputs[1, t, :, at] = x
                spread(x_refs, t, j, 0)
                spread(x_refs, t, j, 1)

            return total, u

        total, u = lax.fori_loop(
            0,
            ring,
            take,
            (jnp.zeros((ROWS, 128), F32), jnp.zeros((ROWS, w_in.shape[0]), F32)),
        )
        total = jnp.sum(total, axis=1, keepdims=True)
        r = lax.rsqrt(total * inv_width + 1e-05)
        u = u * r
        a = gelu(u).astype(BF16)

        @pl.when(last)
        def _():
            u_back[t] = u
            r_back[t] = jnp.broadcast_to(r, (ROWS, 128))
            a_back[t] = a
            slope_back[t] = gelu_slope(u)
            entry_wait(1, t)

        def give(j, c):
            at = columns(j)
            y = x_now[:, at].astype(F32) + dot_plain(a, w_out[:, at])
            y_send[t, :, at] = y.astype(BF16)
            if t < TICKS - 1:

                @pl.when(not_last)
                def _():
                    y_copy(t, j).start()

            @pl.when(last)
            def _():
                g = (y - targets[t, :, at].astype(F32)).astype(BF16)
                if t == 0:
                    g_all[t, :, at] = g
                else:
                    d_recv[t - 1, :, at] = g

            return c

        lax.fori_loop(0, ring, give, 0)
        if t == TICKS - 1:
            pltpu.make_async_copy(y_send.at[t], fwd_out, out_sem.at[0]).start()

    def prepare_backward():
        def take(j, c):
            total, u = c
            at = columns(j)
            x = inputs[0, :, :, at].reshape(TICKS * ROWS, cut)
            return total + lane_sums(x), u + dot_last(x, wg[:, at])

        total, u = lax.fori_loop(
            0,
            ring,
            take,
            (
                jnp.zeros((TICKS * ROWS, 128), F32),
                jnp.zeros((TICKS * ROWS, w_in.shape[0]), F32),
            ),
        )
        total = jnp.sum(total, axis=1, keepdims=True)
        r = lax.rsqrt(total * inv_width + 1e-05)
        u = u * r
        slope_back[...] = gelu_slope(u).reshape(slope_back.shape)
        u_back[...] = u.reshape(u_back.shape)
        r_back[...] = jnp.broadcast_to(r, (TICKS * ROWS, 128)).reshape(r_back.shape)
        a_back[...] = gelu(u).astype(BF16).reshape(a_back.shape)

    def spread_later(t):
        for slot in ((), (0,), (1,), (2, 3))[t]:
            spread_all(g_refs, slot, 1)

        @pl.when(not_last)
        def _():
            for slot in ((0,), (1,), (2,), (3,))[t]:
                spread_all(x_refs, slot, 1, act_hbm)

    def backward_take(t):
        row = bwd_rows[0, t]
        used = jnp.where(last, t, row)

        def take(j, c):
            at = columns(j)

            cache, limit = grad[row, :, at], lim_grad[t, :, at]
            if t == 0:

                @pl.when(not_last)
                def _():
                    g_all[t, :, at] = scaled(cache, limit, bwd_code[:, at])

                g = g_all[t, :, at]
            else:

                @pl.when(not_last)
                def _():
                    d_copy(t - 1, j).wait_recv()

                g = clipped(cache, limit, d_recv[t - 1, :, at])
                g_all[t, :, at] = g
            if t < TICKS - 1:
                spread(g_refs, t, j, 0)
            return c + dot_last(g, w_out[:, at])

        d_active = lax.fori_loop(
            0, ring, take, jnp.zeros((ROWS, w_in.shape[0]), F32)
        )
        if t < TICKS - 1:
            spread_later(t)
        u = u_back[used]
        r = r_back[used][:, :1]
        du = d_active * slope_back[used]
        shift = r * r * (jnp.sum(du * u, axis=1, keepdims=True) * inv_width)
        du_tick[t] = (du * r).astype(BF16)
        factors[1, t] = a_back[used]
        return used, r, shift, du.astype(BF16)

    def backward_give(t, held):
        used, r, shift, du = held

        def give(j, c):
            at = columns(j)
            dx = (
                g_all[t, :, at].astype(F32)
                + r * dot_plain(du, wg[:, at])
                - inputs[x_from, used, :, at].astype(F32) * shift
            )
            d_send[t, :, at] = dx.astype(BF16)
            if t < TICKS - 1:

                @pl.when(not_first)
                def _():
                    d_copy(t, j).start()

            return c

        lax.fori_loop(0, ring, give, 0)
        if t == TICKS - 1:
            pltpu.make_async_copy(d_send.at[t], bwd_out, out_sem.at[1]).start()

    def factor_copy(to, frm):
        return pltpu.make_async_remote_copy(
            src_ref=factors,
            dst_ref=f_gather.at[frm],
            send_sem=f_send_sem.at[to],
            recv_sem=f_recv_sem.at[frm],
            device_id={"dp": to * 2 + py},
            device_id_type=MESH,
        )

    def backward(t):
        backward_give(t, backward_take(t))

    def send_factors():
        used = [jnp.where(last, t, bwd_rows[0, t]) for t in range(TICKS)]
        for q in range(TICKS):
            at = 0
            for t in range(1, TICKS):
                at = jnp.where(used[t] == q, t, at)
            factors[0, q] = du_tick[at]
        for k in range(1, ring):
            factor_copy(lax.rem(px + k, ring), px).start()
        pltpu.make_async_copy(factors, f_gather.at[px], f_recv_sem.at[px]).start()

    rows = ring * TICKS * ROWS
    win = w_in.shape[0]

    def product(which, half):
        at = pl.ds(pl.multiple_of(half * share, 128), share)
        data = (x_gather, g_gather)[which]
        return dot_first(
            f_gather[:, which].reshape(rows, win),
            data[:, :, :, at].reshape(rows, share),
        )

    def swap(which):
        return pltpu.make_async_remote_copy(
            src_ref=p_send.at[which],
            dst_ref=p_recv.at[which],
            send_sem=p_send_sem.at[which],
            recv_sem=p_recv_sem.at[which],
            device_id={"dp": mate},
            device_id_type=MESH,
        )

    def give_product(which):
        p_send[which] = product(which, 1 - py).astype(BF16)
        swap(which).start()

    def spread_last_gradient():
        spread_all(g_refs, TICKS - 1, 0)
        spread_later(TICKS - 1)

    def first_products():
        pltpu.make_async_copy(factors, f_gather.at[px], f_recv_sem.at[px]).wait()
        for k in range(1, ring):
            other = lax.rem(px + k, ring)
            factor_copy(other, other).wait()
        spread_wait(x_refs, 0)
        give_product(0)

    def second_products():
        spread_wait(g_refs, 0)
        give_product(1)

    def rest_of_limits():
        def one(t, c):
            expand_forward(t)
            expand_backward(t)
            return c

        lax.fori_loop(1, TICKS, one, 0)

        @pl.when(last)
        def _():
            for t in range(1, TICKS):
                lim_grad[t] = jnp.full((ROWS, width), OPEN, BF16)

    def more_entries(t):
        start_entries(t, 0)
        start_entries(t, 1)

    @pl.when(last)
    def _():
        for i in (2, 3, 4, 5):
            loads[i].wait()
        expand_forward(0)
        forward(0)
        backward(0)
        more_entries(2)
        more_entries(3)
        rest_of_limits()
        for t in range(1, TICKS - 1):
            forward(t)
            backward(t)
        forward(TICKS - 1)
        held = backward_take(TICKS - 1)
        send_factors()
        spread_last_gradient()
        backward_give(TICKS - 1, held)
        first_products()
        second_products()

    @pl.when(not_last)
    def _():
        @pl.when(s % 2 == 1)
        def _():
            for i in (2, 3):
                loads[i].wait()
            expand_forward(0)
            forward(0)
            for i in (4, 5):
                loads[i].wait()
            prepare_backward()
            expand_backward(0)
            backward(0)

        @pl.when(s % 2 == 0)
        def _():
            for i in (4, 5, 3):
                loads[i].wait()
            prepare_backward()
            expand_backward(0)
            backward(0)
            loads[2].wait()
            expand_forward(0)
            forward(0)

        more_entries(2)
        more_entries(3)
        rest_of_limits()

        @pl.when(s % 2 == 1)
        def _():
            forward(1)
            backward(1)

        @pl.when(s % 2 == 0)
        def _():
            backward(1)
            forward(1)

        backward(2)
        forward(2)

        @pl.when(s % 2 == 1)
        def _():
            forward(TICKS - 1)

        held = backward_take(TICKS - 1)
        send_factors()
        spread_last_gradient()
        backward_give(TICKS - 1, held)
        first_products()
        second_products()

        @pl.when(s % 2 == 0)
        def _():
            forward(TICKS - 1)


    factor = 1.0 / (TICKS * replicas)
    at = pl.ds(pl.multiple_of(p * share, 128), share)
    spread_wait(x_refs, 1)
    own = product(0, py)
    swap(0).wait()
    total = own + p_recv[0].astype(F32)
    gw_in_out[...] = (total * (gain_ref[:, at].astype(F32) * factor)).astype(BF16)
    ggain_out[...] = (
        jnp.sum(total * w_in[:, at].astype(F32), axis=0, keepdims=True) * factor
    )
    spread_wait(g_refs, 1)
    own = product(1, py)
    swap(1).wait()
    gw_out_out[...] = ((own + p_recv[1].astype(F32)) * factor).astype(BF16)

    for t in range(TICKS):
        for which, away, _ in ends:

            @pl.when(away)
            def _():
                entry_copy(which, t, 0).wait_send()
                entry_copy(which, t, 1).wait_send()

    for t in range(TICKS - 1):
        for j in range(ring):

            @pl.when(not_last)
            def _():
                y_copy(t, j).wait_send()

            @pl.when(not_first)
            def _():
                d_copy(t, j).wait_send()

    pltpu.make_async_copy(y_send.at[TICKS - 1], fwd_out, out_sem.at[0]).wait()
    pltpu.make_async_copy(d_send.at[TICKS - 1], bwd_out, out_sem.at[1]).wait()


def hand_over(*refs):
    sources, results, held, sem = refs[:5], refs[5:10], refs[10:15], refs[15]
    takes = [
        pltpu.make_async_copy(src, mid, sem.at[0, i])
        for i, (src, mid) in enumerate(zip(sources, held))
    ]
    gives = [
        pltpu.make_async_copy(mid, dst, sem.at[1, i])
        for i, (mid, dst) in enumerate(zip(held, results))
    ]
    for take in takes:
        take.start()
    for take, give in zip(takes, gives):
        take.wait()
        give.start()
    for give in gives:
        give.wait()


def solution(mesh):
    sections = mesh.shape["section"]
    replicas = mesh.shape["dp"]

    def body(
        entry_codes,
        loss_target,
        fwd_inflow,
        bwd_inflow,
        act_cache,
        act_exps,
        grad_cache,
        grad_exps,
        fwd_rows,
        bwd_rows,
        norm_gain,
        w_in,
        w_out,
    ):
        win, width = w_in.shape[1:]
        ring = replicas // 2
        cut = width // ring
        share = width // replicas
        blocks = act_exps.shape[-1]
        full = (ROWS, width)
        dma = pltpu.SemaphoreType.DMA
        hbm = pl.BlockSpec(memory_space=pltpu.HBM)
        vmem = pl.BlockSpec(memory_space=pltpu.VMEM)
        outs = pl.pallas_call(
            functools.partial(kernel, sections, replicas),
            out_shape=(
                jax.ShapeDtypeStruct((win, share), BF16),
                jax.ShapeDtypeStruct((win, share), BF16),
                jax.ShapeDtypeStruct((1, share), F32),
                jax.ShapeDtypeStruct(full, BF16),
                jax.ShapeDtypeStruct(full, BF16),
            ),
            in_specs=[hbm] * 13,
            out_specs=(vmem, vmem, vmem, hbm, hbm),
            scratch_shapes=[
                pltpu.SMEM((1, TICKS), jnp.int32),
                pltpu.SMEM((1, TICKS), jnp.int32),
                pltpu.VMEM((1, width), BF16),
                pltpu.VMEM((TICKS, ROWS, blocks), jnp.int32),
                pltpu.VMEM((TICKS, ROWS, blocks), jnp.int32),
                pltpu.VMEM((2, TICKS) + full, BF16),
                pltpu.VMEM((TICKS,) + full, BF16),
                pltpu.VMEM((win, width), BF16),
                pltpu.VMEM((win, width), BF16),
                pltpu.VMEM((win, width), BF16),
                pltpu.VMEM(full, BF16),
                pltpu.VMEM(full, BF16),
                pltpu.VMEM((TICKS,) + full, BF16),
                pltpu.VMEM((TICKS,) + full, BF16),
                pltpu.VMEM((TICKS,) + full, BF16),
                pltpu.VMEM((TICKS,) + full, BF16),
                pltpu.VMEM(full, BF16),
                pltpu.VMEM((TICKS,) + full, BF16),
                pltpu.VMEM((TICKS,) + full, BF16),
                pltpu.VMEM((TICKS - 1,) + full, BF16),
                pltpu.VMEM((TICKS,) + full, BF16),
                pltpu.VMEM((TICKS - 1,) + full, BF16),
                pltpu.VMEM((TICKS, ROWS, win), F32),
                pltpu.VMEM((TICKS, ROWS, win), F32),
                pltpu.VMEM((TICKS, ROWS, 128), F32),
                pltpu.VMEM((TICKS, ROWS, win), BF16),
                pltpu.VMEM((TICKS, ROWS, win), BF16),
                pltpu.VMEM((2, TICKS, ROWS, win), BF16),
                pltpu.VMEM((ring, TICKS, ROWS, cut), BF16),
                pltpu.VMEM((ring, TICKS, ROWS, cut), BF16),
                pltpu.VMEM((ring, 2, TICKS, ROWS, win), BF16),
                pltpu.VMEM((2, win, share), BF16),
                pltpu.VMEM((2, win, share), BF16),
                dma((11,)),
                pltpu.VMEM((TICKS, ROWS, width // sections), BF16),
                dma((2, 2)),
                dma((2, TICKS)),
                dma((2, TICKS)),
                dma((TICKS - 1, ring)),
                dma((TICKS - 1, ring)),
                dma((TICKS - 1, ring)),
                dma((TICKS - 1, ring)),
                dma((2 * TICKS, ring)),
                dma((ring, 2 * TICKS)),
                dma((2 * TICKS, ring)),
                dma((ring, 2 * TICKS)),
                dma((ring,)),
                dma((ring,)),
                dma((2,)),
                dma((2,)),
                dma((2,)),
            ],
            compiler_params=pltpu.CompilerParams(
                collective_id=0,
                has_side_effects=True,
                vmem_limit_bytes=VMEM_BYTES,
            ),
        )(
            fwd_rows,
            bwd_rows,
            norm_gain,
            act_exps[0],
            grad_exps[0],
            entry_codes,
            loss_target,
            fwd_inflow[0],
            bwd_inflow[0],
            act_cache[0],
            grad_cache[0],
            w_in[0],
            w_out[0],
        )
        gw_in, gw_out, ggain, fwd_last, bwd_last = pl.pallas_call(
            hand_over,
            out_shape=tuple(jax.ShapeDtypeStruct(o.shape, o.dtype) for o in outs),
            in_specs=[pl.BlockSpec(memory_space=pl.ANY)] * 5,
            out_specs=(hbm,) * 5,
            scratch_shapes=[pltpu.VMEM(o.shape, o.dtype) for o in outs] + [dma((2, 5))],
            compiler_params=pltpu.CompilerParams(vmem_limit_bytes=VMEM_BYTES),
        )(*outs)
        return gw_in[None], gw_out[None], ggain, fwd_last[None], bwd_last[None]

    return jax.shard_map(
        body,
        mesh=mesh,
        in_specs=(
            P(None, "dp", "section"),
            P(None, "dp", "section"),
            P("section", "dp", None),
            P("section", "dp", None),
            P("section", "dp", None, None),
            P("section", "dp", None, None),
            P("section", "dp", None, None),
            P("section", "dp", None, None),
            P("section", "dp"),
            P("section", "dp"),
            P("section", None),
            P("section", None, None),
            P("section", None, None),
        ),
        out_specs=(
            P("section", None, "dp"),
            P("section", None, "dp"),
            P("section", "dp"),
            P("section", "dp", None),
            P("section", "dp", None),
        ),
        check_vma=False,
    )
```

```python
import functools

import jax
import jax.numpy as jnp
from jax import lax
from jax.experimental import pallas as pl
from jax.experimental.pallas import tpu as pltpu
from jax.sharding import PartitionSpec as P

MESH = pl.DeviceIdType.MESH
ROWS = 16
TICKS = 4
VMEM_BYTES = 64 * 1024 * 1024
OPEN = 3e38
F32 = jnp.float32
BF16 = jnp.bfloat16


def dot_last(a, b):
    return lax.dot_general(a, b, (((1,), (1,)), ((), ())), preferred_element_type=F32)


def dot_first(a, b):
    return lax.dot_general(a, b, (((0,), (0,)), ((), ())), preferred_element_type=F32)


def dot_plain(a, b):
    return lax.dot_general(a, b, (((1,), (0,)), ((), ())), preferred_element_type=F32)


def lane_sums(x):
    x = x.astype(F32)
    x = x * x
    return sum(x[:, i : i + 128] for i in range(0, x.shape[1], 128))


def half_erf(u):
    return 0.5 * (1.0 + lax.erf(u * 0.7071067811865476))


def gelu(u):
    return u * half_erf(u)


def gelu_slope(u):
    return half_erf(u) + u * jnp.exp(-0.5 * u * u) * 0.3989422804014327


def kernel(
    sections,
    replicas,
    fwd_rows_hbm,
    bwd_rows_hbm,
    gain_hbm,
    act_exps_hbm,
    grad_exps_hbm,
    entry_hbm,
    target_hbm,
    fwd_inflow,
    bwd_inflow,
    act_hbm,
    grad_hbm,
    w_in_hbm,
    w_out_hbm,
    gw_in_out,
    gw_out_out,
    ggain_out,
    fwd_out,
    bwd_out,
    fwd_rows,
    bwd_rows,
    gain_ref,
    act_exps,
    grad_exps,
    inputs,
    grad,
    w_in,
    w_out,
    wg,
    fwd_code,
    bwd_code,
    entries,
    targets,
    lim_act,
    lim_grad,
    x_now,
    g_all,
    y_send,
    y_recv,
    d_send,
    d_recv,
    u_back,
    slope_back,
    r_back,
    a_back,
    du_tick,
    factors,
    x_gather,
    g_gather,
    f_gather,
    p_send,
    p_recv,
    load_sem,
    mail,
    mail_sem,
    entry_send,
    entry_recv,
    y_send_sem,
    y_recv_sem,
    d_send_sem,
    d_recv_sem,
    x_send_sem,
    x_recv_sem,
    g_send_sem,
    g_recv_sem,
    f_send_sem,
    f_recv_sem,
    p_send_sem,
    p_recv_sem,
    out_sem,
):
    width = w_in.shape[1]
    ring = replicas // 2
    cut = width // ring
    share = width // replicas
    piece = width // sections
    inv_width = 1.0 / width
    act = inputs.at[0]
    s = lax.axis_index("section")
    p = lax.axis_index("dp")
    px = p // 2
    py = p % 2
    first = s == 0
    last = s == sections - 1
    x_from = jnp.where(last, 1, 0)
    not_first = s > 0
    not_last = s < sections - 1
    mate = px * 2 + (1 - py)
    side = s // 2 % 2
    partner = s + 2 - 4 * side

    barrier = pltpu.get_barrier_semaphore()

    def greet(where):
        pl.semaphore_signal(barrier, inc=1, device_id=where, device_id_type=MESH)

    @pl.when(not_first)
    def _():
        greet({"section": s - 1})

    @pl.when(not_last)
    def _():
        greet({"section": s + 1})

    for k in range(1, ring):
        greet({"dp": lax.rem(px + k, ring) * 2 + py})
    greet({"dp": mate})
    greet({"section": partner})

    @pl.when(first)
    def _():
        def tell(i, c):
            greet({"section": i})
            return c

        lax.fori_loop(1, sections, tell, 0)

    @pl.when(last)
    def _():
        def tell(i, c):
            greet({"section": i})
            return c

        lax.fori_loop(0, sections - 1, tell, 0)

    loads = [
        pltpu.make_async_copy(src, dst, load_sem.at[i])
        for i, (src, dst) in enumerate(
            [
                (act_hbm, act),
                (w_in_hbm, w_in),
                (fwd_inflow, fwd_code),
                (w_out_hbm, w_out),
                (grad_hbm, grad),
                (bwd_inflow, bwd_code),
                (fwd_rows_hbm, fwd_rows),
                (bwd_rows_hbm, bwd_rows),
                (gain_hbm, gain_ref),
                (act_exps_hbm, act_exps),
                (grad_exps_hbm, grad_exps),
            ]
        )
    ]
    for i in (9, 10, 8, 6, 7, 1, 0):
        loads[i].start()

    @pl.when(s % 2 == 1)
    def _():
        for i in (2, 3, 4, 5):
            loads[i].start()

    @pl.when(s % 2 == 0)
    def _():
        for i in (4, 5, 3, 2):
            loads[i].start()

    count = (
        jnp.where(not_first, 2, 0) + jnp.where(not_last, 2, 0) + (ring - 1) + 2
    )
    pl.semaphore_wait(barrier, count)

    def mine(owner):
        return pl.ds(pl.multiple_of(owner * piece, 128), piece)

    def mail_copy(src):
        at = pl.ds(1, TICKS - 1)
        return pltpu.make_async_remote_copy(
            src_ref=src.at[at],
            dst_ref=mail.at[at],
            send_sem=mail_sem.at[0],
            recv_sem=mail_sem.at[1],
            device_id={"section": partner},
            device_id_type=MESH,
        )

    def entry_copy(which, t, from_mail):
        src = mail if from_mail else (entry_hbm, target_hbm)[which]
        dst = (entries, targets)[which]
        return pltpu.make_async_remote_copy(
            src_ref=src.at[t],
            dst_ref=dst.at[t, :, mine(partner if from_mail else s)],
            send_sem=entry_send.at[from_mail if t > 0 else which, t],
            recv_sem=entry_recv.at[which, t],
            device_id={"section": (0, sections - 1)[which]},
            device_id_type=MESH,
        )

    def entry_local(which, t, from_mail):
        src = mail if from_mail else (entry_hbm, target_hbm)[which]
        dst = (entries, targets)[which]
        return pltpu.make_async_copy(
            src.at[t],
            dst.at[t, :, mine(partner if from_mail else s)],
            entry_recv.at[which, t],
        )

    def entry_wait(which, t):
        dst = (entries, targets)[which]
        pltpu.make_async_copy(dst.at[t], dst.at[t], entry_recv.at[which, t]).wait()

    direct = ((0, not_first, first), (1, not_last, last))
    ends = ((0, (side == 0) & not_first, first), (1, (side == 1) & not_last, last))

    def start_entries(t, from_mail):
        for which, away, here in direct if t == 0 else ends:

            @pl.when(away)
            def _():
                entry_copy(which, t, from_mail).start()

            @pl.when(here)
            def _():
                entry_local(which, t, from_mail).start()

    start_entries(0, 0)

    @pl.when(side == 0)
    def _():
        mail_copy(target_hbm).start()

    @pl.when(side == 1)
    def _():
        mail_copy(entry_hbm).start()

    def columns(j):
        return pl.ds(pl.multiple_of(j * cut, 128), cut)

    def half_columns(j, part):
        half = 1 - py if part == 0 else py
        return pl.ds(pl.multiple_of(j * cut + half * share, 128), share)

    def spread(refs, slot, j, part, src=None):
        held, dst, send_sem, recv_sem = refs
        src = held if src is None else src
        index = slot * 2 + part

        @pl.when(j != px)
        def _():
            pltpu.make_async_remote_copy(
                src_ref=src.at[slot, :, half_columns(j, part)],
                dst_ref=dst.at[px, slot, :, half_columns(0, part)],
                send_sem=send_sem.at[index, j],
                recv_sem=recv_sem.at[px, index],
                device_id={"dp": j * 2 + py},
                device_id_type=MESH,
            ).start()

        @pl.when(j == px)
        def _():
            pltpu.make_async_copy(
                src.at[slot, :, half_columns(j, part)],
                dst.at[px, slot, :, half_columns(0, part)],
                recv_sem.at[px, index],
            ).start()

    def spread_all(refs, slot, part, src=None):
        for k in range(ring):
            spread(refs, slot, lax.rem(px + k, ring), part, src)

    def spread_wait(refs, part):
        src, dst, send_sem, recv_sem = refs

        def one(i, c):
            slot, k = i // ring, i % ring
            index = slot * 2 + part

            @pl.when(k != px)
            def _():
                copy = pltpu.make_async_remote_copy(
                    src_ref=src.at[slot, :, half_columns(k, part)],
                    dst_ref=dst.at[k, slot, :, half_columns(0, part)],
                    send_sem=send_sem.at[index, k],
                    recv_sem=recv_sem.at[k, index],
                    device_id={"dp": k * 2 + py},
                    device_id_type=MESH,
                )
                copy.wait_recv()
                copy.wait_send()

            @pl.when(k == px)
            def _():
                pltpu.make_async_copy(
                    src.at[slot, :, half_columns(k, part)],
                    dst.at[k, slot, :, half_columns(0, part)],
                    recv_sem.at[k, index],
                ).wait()

            return c

        lax.fori_loop(0, ring * TICKS, one, 0)

    x_refs = (inputs.at[1], x_gather, x_send_sem, x_recv_sem)
    g_refs = (g_all, g_gather, g_send_sem, g_recv_sem)

    @pl.when(not_last)
    def _():
        for slot in range(TICKS):
            spread_all(x_refs, slot, 0, act_hbm)

    blocks = act_exps.shape[-1]

    def expand(exps, rows, limits, t):
        scale = jnp.exp2(exps[rows[0, t]].astype(F32) + 4.0)
        for j in range(ring):
            limits[t, :, j * cut : (j + 1) * cut] = jnp.concatenate(
                [
                    jnp.broadcast_to(scale[:, b : b + 1], (ROWS, 128))
                    for b in range(j * blocks // ring, (j + 1) * blocks // ring)
                ],
                axis=1,
            ).astype(BF16)

    def expand_forward(t):
        expand(act_exps, fwd_rows, lim_act, t)

    def expand_backward(t):
        expand(grad_exps, bwd_rows, lim_grad, t)

    loads[1].wait()
    loads[8].wait()

    def fold(j, c):
        wg[:, columns(j)] = (
            w_in[:, columns(j)].astype(F32) * gain_ref[:, columns(j)].astype(F32)
        ).astype(BF16)
        return c

    lax.fori_loop(0, ring, fold, 0)

    def pass_entries():
        start_entries(1, 0)
        mail_copy(target_hbm).wait()
        start_entries(1, 1)

    @pl.when(last)
    def _():
        pass_entries()
    for i in (0, 6, 7, 9, 10):
        loads[i].wait()

    def y_copy(t, j):
        return pltpu.make_async_remote_copy(
            src_ref=y_send.at[t, :, columns(j)],
            dst_ref=y_recv.at[t, :, columns(j)],
            send_sem=y_send_sem.at[t, j],
            recv_sem=y_recv_sem.at[t, j],
            device_id={"section": s + 1},
            device_id_type=MESH,
        )

    def d_copy(t, j):
        return pltpu.make_async_remote_copy(
            src_ref=d_send.at[t, :, columns(j)],
            dst_ref=d_recv.at[t, :, columns(j)],
            send_sem=d_send_sem.at[t, j],
            recv_sem=d_recv_sem.at[t, j],
            device_id={"section": s - 1},
            device_id_type=MESH,
        )

    def scaled(cache, limit, code):
        return (
            cache.astype(F32) + limit.astype(F32) * 0.0625 * code.astype(F32)
        ).astype(BF16)

    def clipped(cache, limit, value):
        return jnp.minimum(jnp.maximum(value, cache - limit), cache + limit)

    def forward(t):
        row = fwd_rows[0, t]

        @pl.when(first)
        def _():
            entry_wait(0, t)
            if t > 0:
                y_recv[t - 1] = scaled(act[row], lim_act[t], entries[t])
                lim_act[t] = jnp.full((ROWS, width), OPEN, BF16)

        def take(j, c):
            total, u = c
            at = columns(j)
            cache, limit = act[row, :, at], lim_act[t, :, at]
            if t == 0:

                @pl.when(first)
                def _():
                    x_now[:, at] = scaled(cache, limit, entries[t, :, at])

                @pl.when(not_first)
                def _():
                    x_now[:, at] = scaled(cache, limit, fwd_code[:, at])

                x = x_now[:, at]
            else:

                @pl.when(not_first)
                def _():
                    y_copy(t - 1, j).wait_recv()

                x = clipped(cache, limit, y_recv[t - 1, :, at])
                x_now[:, at] = x

            total = total + lane_sums(x)
            u = u + dot_last(x, wg[:, at])

            @pl.when(last)
            def _():
                inputs[1, t, :, at] = x
                spread(x_refs, t, j, 0)
                spread(x_refs, t, j, 1)

            return total, u

        total, u = lax.fori_loop(
            0,
            ring,
            take,
            (jnp.zeros((ROWS, 128), F32), jnp.zeros((ROWS, w_in.shape[0]), F32)),
        )
        total = jnp.sum(total, axis=1, keepdims=True)
        r = lax.rsqrt(total * inv_width + 1e-05)
        u = u * r
        a = gelu(u).astype(BF16)

        @pl.when(last)
        def _():
            u_back[t] = u
            r_back[t] = jnp.broadcast_to(r, (ROWS, 128))
            a_back[t] = a
            slope_back[t] = gelu_slope(u)
            entry_wait(1, t)

        def give(j, c):
            at = columns(j)
            y = x_now[:, at].astype(F32) + dot_plain(a, w_out[:, at])
            y_send[t, :, at] = y.astype(BF16)
            if t < TICKS - 1:

                @pl.when(not_last)
                def _():
                    y_copy(t, j).start()

            @pl.when(last)
            def _():
                g = (y - targets[t, :, at].astype(F32)).astype(BF16)
                if t == 0:
                    g_all[t, :, at] = g
                else:
                    d_recv[t - 1, :, at] = g

            return c

        lax.fori_loop(0, ring, give, 0)
        if t == TICKS - 1:
            pltpu.make_async_copy(y_send.at[t], fwd_out, out_sem.at[0]).start()

    def prepare_backward():
        def take(j, c):
            total, u = c
            at = columns(j)
            x = inputs[0, :, :, at].reshape(TICKS * ROWS, cut)
            return total + lane_sums(x), u + dot_last(x, wg[:, at])

        total, u = lax.fori_loop(
            0,
            ring,
            take,
            (
                jnp.zeros((TICKS * ROWS, 128), F32),
                jnp.zeros((TICKS * ROWS, w_in.shape[0]), F32),
            ),
        )
        total = jnp.sum(total, axis=1, keepdims=True)
        r = lax.rsqrt(total * inv_width + 1e-05)
        u = u * r
        slope_back[...] = gelu_slope(u).reshape(slope_back.shape)
        u_back[...] = u.reshape(u_back.shape)
        r_back[...] = jnp.broadcast_to(r, (TICKS * ROWS, 128)).reshape(r_back.shape)
        a_back[...] = gelu(u).astype(BF16).reshape(a_back.shape)

    def spread_later(t):
        for slot in ((), (0,), (1,), (2, 3))[t]:
            spread_all(g_refs, slot, 1)

        @pl.when(not_last)
        def _():
            for slot in ((0,), (1,), (2,), (3,))[t]:
                spread_all(x_refs, slot, 1, act_hbm)

    def backward_take(t):
        row = bwd_rows[0, t]
        used = jnp.where(last, t, row)

        def take(j, c):
            at = columns(j)

            cache, limit = grad[row, :, at], lim_grad[t, :, at]
            if t == 0:

                @pl.when(not_last)
                def _():
                    g_all[t, :, at] = scaled(cache, limit, bwd_code[:, at])

                g = g_all[t, :, at]
            else:

                @pl.when(not_last)
                def _():
                    d_copy(t - 1, j).wait_recv()

                g = clipped(cache, limit, d_recv[t - 1, :, at])
                g_all[t, :, at] = g
            if t < TICKS - 1:
                spread(g_refs, t, j, 0)
            return c + dot_last(g, w_out[:, at])

        d_active = lax.fori_loop(
            0, ring, take, jnp.zeros((ROWS, w_in.shape[0]), F32)
        )
        if t < TICKS - 1:
            spread_later(t)
        u = u_back[used]
        r = r_back[used][:, :1]
        du = d_active * slope_back[used]
        shift = r * r * (jnp.sum(du * u, axis=1, keepdims=True) * inv_width)
        du_tick[t] = (du * r).astype(BF16)
        factors[1, t] = a_back[used]
        return used, r, shift, du.astype(BF16)

    def backward_give(t, held):
        used, r, shift, du = held

        def give(j, c):
            at = columns(j)
            dx = (
                g_all[t, :, at].astype(F32)
                + r * dot_plain(du, wg[:, at])
                - inputs[x_from, used, :, at].astype(F32) * shift
            )
            d_send[t, :, at] = dx.astype(BF16)
            if t < TICKS - 1:

                @pl.when(not_first)
                def _():
                    d_copy(t, j).start()

            return c

        lax.fori_loop(0, ring, give, 0)
        if t == TICKS - 1:
            pltpu.make_async_copy(d_send.at[t], bwd_out, out_sem.at[1]).start()

    def factor_copy(to, frm):
        return pltpu.make_async_remote_copy(
            src_ref=factors,
            dst_ref=f_gather.at[frm],
            send_sem=f_send_sem.at[to],
            recv_sem=f_recv_sem.at[frm],
            device_id={"dp": to * 2 + py},
            device_id_type=MESH,
        )

    def backward(t):
        backward_give(t, backward_take(t))

    def send_factors():
        used = [jnp.where(last, t, bwd_rows[0, t]) for t in range(TICKS)]
        for q in range(TICKS):
            at = 0
            for t in range(1, TICKS):
                at = jnp.where(used[t] == q, t, at)
            factors[0, q] = du_tick[at]
        for k in range(1, ring):
            factor_copy(lax.rem(px + k, ring), px).start()
        pltpu.make_async_copy(factors, f_gather.at[px], f_recv_sem.at[px]).start()

    rows = ring * TICKS * ROWS
    win = w_in.shape[0]

    def product(which, half):
        at = pl.ds(pl.multiple_of(half * share, 128), share)
        data = (x_gather, g_gather)[which]
        return dot_first(
            f_gather[:, which].reshape(rows, win),
            data[:, :, :, at].reshape(rows, share),
        )

    def swap(which):
        return pltpu.make_async_remote_copy(
            src_ref=p_send.at[which],
            dst_ref=p_recv.at[which],
            send_sem=p_send_sem.at[which],
            recv_sem=p_recv_sem.at[which],
            device_id={"dp": mate},
            device_id_type=MESH,
        )

    def give_product(which):
        p_send[which] = product(which, 1 - py).astype(BF16)
        swap(which).start()

    def spread_last_gradient():
        spread_all(g_refs, TICKS - 1, 0)
        spread_later(TICKS - 1)

    def first_products():
        pltpu.make_async_copy(factors, f_gather.at[px], f_recv_sem.at[px]).wait()
        for k in range(1, ring):
            other = lax.rem(px + k, ring)
            factor_copy(other, other).wait()
        spread_wait(x_refs, 0)
        give_product(0)

    def second_products():
        spread_wait(g_refs, 0)
        give_product(1)

    def rest_of_limits():
        def one(t, c):
            expand_forward(t)
            expand_backward(t)
            return c

        lax.fori_loop(1, TICKS, one, 0)

        @pl.when(last)
        def _():
            for t in range(1, TICKS):
                lim_grad[t] = jnp.full((ROWS, width), OPEN, BF16)

    def more_entries(t):
        start_entries(t, 0)
        start_entries(t, 1)

    @pl.when(last)
    def _():
        for i in (2, 3, 4, 5):
            loads[i].wait()
        expand_forward(0)
        forward(0)
        backward(0)
        more_entries(2)
        more_entries(3)
        rest_of_limits()
        for t in range(1, TICKS - 1):
            forward(t)
            backward(t)
        forward(TICKS - 1)
        held = backward_take(TICKS - 1)
        send_factors()
        spread_last_gradient()
        backward_give(TICKS - 1, held)
        first_products()
        second_products()

    @pl.when(not_last)
    def _():
        @pl.when(s % 2 == 1)
        def _():
            for i in (2, 3):
                loads[i].wait()
            expand_forward(0)
            forward(0)
            pass_entries()
            for i in (4, 5):
                loads[i].wait()
            prepare_backward()
            expand_backward(0)
            backward(0)

        @pl.when(s % 2 == 0)
        def _():
            for i in (4, 5, 3):
                loads[i].wait()
            prepare_backward()
            expand_backward(0)
            backward(0)
            pass_entries()
            loads[2].wait()
            expand_forward(0)
            forward(0)

        more_entries(2)
        more_entries(3)
        rest_of_limits()

        @pl.when(s % 2 == 1)
        def _():
            forward(1)
            backward(1)

        @pl.when(s % 2 == 0)
        def _():
            backward(1)
            forward(1)

        backward(2)
        forward(2)

        @pl.when(s % 2 == 1)
        def _():
            forward(TICKS - 1)

        held = backward_take(TICKS - 1)
        send_factors()
        spread_last_gradient()
        backward_give(TICKS - 1, held)
        first_products()
        second_products()

        @pl.when(s % 2 == 0)
        def _():
            forward(TICKS - 1)


    factor = 1.0 / (TICKS * replicas)
    at = pl.ds(pl.multiple_of(p * share, 128), share)
    spread_wait(x_refs, 1)
    own = product(0, py)
    swap(0).wait()
    total = own + p_recv[0].astype(F32)
    gw_in_out[...] = (total * (gain_ref[:, at].astype(F32) * factor)).astype(BF16)
    ggain_out[...] = (
        jnp.sum(total * w_in[:, at].astype(F32), axis=0, keepdims=True) * factor
    )
    spread_wait(g_refs, 1)
    own = product(1, py)
    swap(1).wait()
    gw_out_out[...] = ((own + p_recv[1].astype(F32)) * factor).astype(BF16)

    for t in range(TICKS):
        for which, away, _ in direct if t == 0 else ends:

            @pl.when(away)
            def _():
                entry_copy(which, t, 0).wait_send()
                if t > 0:
                    entry_copy(which, t, 1).wait_send()

    for t in range(TICKS - 1):
        for j in range(ring):

            @pl.when(not_last)
            def _():
                y_copy(t, j).wait_send()

            @pl.when(not_first)
            def _():
                d_copy(t, j).wait_send()

    pltpu.make_async_copy(y_send.at[TICKS - 1], fwd_out, out_sem.at[0]).wait()
    pltpu.make_async_copy(d_send.at[TICKS - 1], bwd_out, out_sem.at[1]).wait()


def hand_over(*refs):
    sources, results, held, sem = refs[:5], refs[5:10], refs[10:15], refs[15]
    takes = [
        pltpu.make_async_copy(src, mid, sem.at[0, i])
        for i, (src, mid) in enumerate(zip(sources, held))
    ]
    gives = [
        pltpu.make_async_copy(mid, dst, sem.at[1, i])
        for i, (mid, dst) in enumerate(zip(held, results))
    ]
    for take in takes:
        take.start()
    for take, give in zip(takes, gives):
        take.wait()
        give.start()
    for give in gives:
        give.wait()


def solution(mesh):
    sections = mesh.shape["section"]
    replicas = mesh.shape["dp"]

    def body(
        entry_codes,
        loss_target,
        fwd_inflow,
        bwd_inflow,
        act_cache,
        act_exps,
        grad_cache,
        grad_exps,
        fwd_rows,
        bwd_rows,
        norm_gain,
        w_in,
        w_out,
    ):
        win, width = w_in.shape[1:]
        ring = replicas // 2
        cut = width // ring
        share = width // replicas
        blocks = act_exps.shape[-1]
        full = (ROWS, width)
        dma = pltpu.SemaphoreType.DMA
        hbm = pl.BlockSpec(memory_space=pltpu.HBM)
        vmem = pl.BlockSpec(memory_space=pltpu.VMEM)
        outs = pl.pallas_call(
            functools.partial(kernel, sections, replicas),
            out_shape=(
                jax.ShapeDtypeStruct((win, share), BF16),
                jax.ShapeDtypeStruct((win, share), BF16),
                jax.ShapeDtypeStruct((1, share), F32),
                jax.ShapeDtypeStruct(full, BF16),
                jax.ShapeDtypeStruct(full, BF16),
            ),
            in_specs=[hbm] * 13,
            out_specs=(vmem, vmem, vmem, hbm, hbm),
            scratch_shapes=[
                pltpu.SMEM((1, TICKS), jnp.int32),
                pltpu.SMEM((1, TICKS), jnp.int32),
                pltpu.VMEM((1, width), BF16),
                pltpu.VMEM((TICKS, ROWS, blocks), jnp.int32),
                pltpu.VMEM((TICKS, ROWS, blocks), jnp.int32),
                pltpu.VMEM((2, TICKS) + full, BF16),
                pltpu.VMEM((TICKS,) + full, BF16),
                pltpu.VMEM((win, width), BF16),
                pltpu.VMEM((win, width), BF16),
                pltpu.VMEM((win, width), BF16),
                pltpu.VMEM(full, BF16),
                pltpu.VMEM(full, BF16),
                pltpu.VMEM((TICKS,) + full, BF16),
                pltpu.VMEM((TICKS,) + full, BF16),
                pltpu.VMEM((TICKS,) + full, BF16),
                pltpu.VMEM((TICKS,) + full, BF16),
                pltpu.VMEM(full, BF16),
                pltpu.VMEM((TICKS,) + full, BF16),
                pltpu.VMEM((TICKS,) + full, BF16),
                pltpu.VMEM((TICKS - 1,) + full, BF16),
                pltpu.VMEM((TICKS,) + full, BF16),
                pltpu.VMEM((TICKS - 1,) + full, BF16),
                pltpu.VMEM((TICKS, ROWS, win), F32),
                pltpu.VMEM((TICKS, ROWS, win), F32),
                pltpu.VMEM((TICKS, ROWS, 128), F32),
                pltpu.VMEM((TICKS, ROWS, win), BF16),
                pltpu.VMEM((TICKS, ROWS, win), BF16),
                pltpu.VMEM((2, TICKS, ROWS, win), BF16),
                pltpu.VMEM((ring, TICKS, ROWS, cut), BF16),
                pltpu.VMEM((ring, TICKS, ROWS, cut), BF16),
                pltpu.VMEM((ring, 2, TICKS, ROWS, win), BF16),
                pltpu.VMEM((2, win, share), BF16),
                pltpu.VMEM((2, win, share), BF16),
                dma((11,)),
                pltpu.VMEM((TICKS, ROWS, width // sections), BF16),
                dma((2,)),
                dma((2, TICKS)),
                dma((2, TICKS)),
                dma((TICKS - 1, ring)),
                dma((TICKS - 1, ring)),
                dma((TICKS - 1, ring)),
                dma((TICKS - 1, ring)),
                dma((2 * TICKS, ring)),
                dma((ring, 2 * TICKS)),
                dma((2 * TICKS, ring)),
                dma((ring, 2 * TICKS)),
                dma((ring,)),
                dma((ring,)),
                dma((2,)),
                dma((2,)),
                dma((2,)),
            ],
            compiler_params=pltpu.CompilerParams(
                collective_id=0,
                has_side_effects=True,
                vmem_limit_bytes=VMEM_BYTES,
            ),
        )(
            fwd_rows,
            bwd_rows,
            norm_gain,
            act_exps[0],
            grad_exps[0],
            entry_codes,
            loss_target,
            fwd_inflow[0],
            bwd_inflow[0],
            act_cache[0],
            grad_cache[0],
            w_in[0],
            w_out[0],
        )
        gw_in, gw_out, ggain, fwd_last, bwd_last = pl.pallas_call(
            hand_over,
            out_shape=tuple(jax.ShapeDtypeStruct(o.shape, o.dtype) for o in outs),
            in_specs=[pl.BlockSpec(memory_space=pl.ANY)] * 5,
            out_specs=(hbm,) * 5,
            scratch_shapes=[pltpu.VMEM(o.shape, o.dtype) for o in outs] + [dma((2, 5))],
            compiler_params=pltpu.CompilerParams(vmem_limit_bytes=VMEM_BYTES),
        )(*outs)
        return gw_in[None], gw_out[None], ggain, fwd_last[None], bwd_last[None]

    return jax.shard_map(
        body,
        mesh=mesh,
        in_specs=(
            P(None, "dp", "section"),
            P(None, "dp", "section"),
            P("section", "dp", None),
            P("section", "dp", None),
            P("section", "dp", None, None),
            P("section", "dp", None, None),
            P("section", "dp", None, None),
            P("section", "dp", None, None),
            P("section", "dp"),
            P("section", "dp"),
            P("section", None),
            P("section", None, None),
            P("section", None, None),
        ),
        out_specs=(
            P("section", None, "dp"),
            P("section", None, "dp"),
            P("section", "dp"),
            P("section", "dp", None),
            P("section", "dp", None),
        ),
        check_vma=False,
    )
```

```python
import functools

import jax
import jax.numpy as jnp
from jax import lax
from jax.experimental import pallas as pl
from jax.experimental.pallas import tpu as pltpu
from jax.sharding import PartitionSpec as P

MESH = pl.DeviceIdType.MESH
ROWS = 16
TICKS = 4
VMEM_BYTES = 64 * 1024 * 1024
OPEN = 3e38
F32 = jnp.float32
BF16 = jnp.bfloat16


def dot_last(a, b):
    return lax.dot_general(a, b, (((1,), (1,)), ((), ())), preferred_element_type=F32)


def dot_first(a, b):
    return lax.dot_general(a, b, (((0,), (0,)), ((), ())), preferred_element_type=F32)


def dot_plain(a, b):
    return lax.dot_general(a, b, (((1,), (0,)), ((), ())), preferred_element_type=F32)


def lane_sums(x):
    x = x.astype(F32)
    x = x * x
    return sum(x[:, i : i + 128] for i in range(0, x.shape[1], 128))


def half_erf(u):
    return 0.5 * (1.0 + lax.erf(u * 0.7071067811865476))


def gelu(u):
    return u * half_erf(u)


def gelu_slope(u):
    return half_erf(u) + u * jnp.exp(-0.5 * u * u) * 0.3989422804014327


def kernel(
    sections,
    replicas,
    fwd_rows_hbm,
    bwd_rows_hbm,
    gain_hbm,
    act_exps_hbm,
    grad_exps_hbm,
    entry_hbm,
    target_hbm,
    fwd_inflow,
    bwd_inflow,
    act_hbm,
    grad_hbm,
    w_in_hbm,
    w_out_hbm,
    gw_in_out,
    gw_out_out,
    ggain_out,
    fwd_out,
    bwd_out,
    fwd_rows,
    bwd_rows,
    gain_ref,
    act_exps,
    grad_exps,
    inputs,
    grad,
    w_in,
    w_out,
    wg,
    fwd_code,
    bwd_code,
    entries,
    targets,
    lim_act,
    lim_grad,
    x_now,
    g_all,
    y_send,
    y_recv,
    d_send,
    d_recv,
    u_back,
    slope_back,
    r_back,
    a_back,
    du_tick,
    factors,
    x_gather,
    g_gather,
    f_gather,
    p_send,
    p_recv,
    load_sem,
    mail,
    mail_sem,
    entry_send,
    entry_recv,
    y_send_sem,
    y_recv_sem,
    d_send_sem,
    d_recv_sem,
    x_send_sem,
    x_recv_sem,
    g_send_sem,
    g_recv_sem,
    f_send_sem,
    f_recv_sem,
    p_send_sem,
    p_recv_sem,
    out_sem,
):
    width = w_in.shape[1]
    ring = replicas // 2
    cut = width // ring
    share = width // replicas
    piece = width // sections
    inv_width = 1.0 / width
    act = inputs.at[0]
    s = lax.axis_index("section")
    p = lax.axis_index("dp")
    px = p // 2
    py = p % 2
    first = s == 0
    last = s == sections - 1
    x_from = jnp.where(last, 1, 0)
    not_first = s > 0
    not_last = s < sections - 1
    mate = px * 2 + (1 - py)
    side = s // 2 % 2
    partner = s + 2 - 4 * side

    barrier = pltpu.get_barrier_semaphore()

    def greet(where):
        pl.semaphore_signal(barrier, inc=1, device_id=where, device_id_type=MESH)

    @pl.when(not_first)
    def _():
        greet({"section": s - 1})

    @pl.when(not_last)
    def _():
        greet({"section": s + 1})

    for k in range(1, ring):
        greet({"dp": lax.rem(px + k, ring) * 2 + py})
    greet({"dp": mate})
    greet({"section": partner})

    @pl.when(first)
    def _():
        def tell(i, c):
            greet({"section": i})
            return c

        lax.fori_loop(1, sections, tell, 0)

    @pl.when(last)
    def _():
        def tell(i, c):
            greet({"section": i})
            return c

        lax.fori_loop(0, sections - 1, tell, 0)

    loads = [
        pltpu.make_async_copy(src, dst, load_sem.at[i])
        for i, (src, dst) in enumerate(
            [
                (act_hbm, act),
                (w_in_hbm, w_in),
                (fwd_inflow, fwd_code),
                (w_out_hbm, w_out),
                (grad_hbm, grad),
                (bwd_inflow, bwd_code),
                (fwd_rows_hbm, fwd_rows),
                (bwd_rows_hbm, bwd_rows),
                (gain_hbm, gain_ref),
                (act_exps_hbm, act_exps),
                (grad_exps_hbm, grad_exps),
            ]
        )
    ]
    for i in (9, 10, 8, 6, 7, 1, 0):
        loads[i].start()

    @pl.when(s % 2 == 1)
    def _():
        for i in (2, 3, 4, 5):
            loads[i].start()

    @pl.when(s % 2 == 0)
    def _():
        for i in (4, 5, 3, 2):
            loads[i].start()

    count = (
        jnp.where(not_first, 2, 0) + jnp.where(not_last, 2, 0) + (ring - 1) + 2
    )
    pl.semaphore_wait(barrier, count)

    def mine(owner):
        return pl.ds(pl.multiple_of(owner * piece, 128), piece)

    def mail_copy(src):
        at = pl.ds(1, TICKS - 1)
        return pltpu.make_async_remote_copy(
            src_ref=src.at[at],
            dst_ref=mail.at[at],
            send_sem=mail_sem.at[0],
            recv_sem=mail_sem.at[1],
            device_id={"section": partner},
            device_id_type=MESH,
        )

    def entry_copy(which, t, from_mail):
        src = mail if from_mail else (entry_hbm, target_hbm)[which]
        dst = (entries, targets)[which]
        return pltpu.make_async_remote_copy(
            src_ref=src.at[t],
            dst_ref=dst.at[t, :, mine(partner if from_mail else s)],
            send_sem=entry_send.at[from_mail if t > 0 else which, t],
            recv_sem=entry_recv.at[which, t],
            device_id={"section": (0, sections - 1)[which]},
            device_id_type=MESH,
        )

    def entry_local(which, t, from_mail):
        src = mail if from_mail else (entry_hbm, target_hbm)[which]
        dst = (entries, targets)[which]
        return pltpu.make_async_copy(
            src.at[t],
            dst.at[t, :, mine(partner if from_mail else s)],
            entry_recv.at[which, t],
        )

    def entry_wait(which, t):
        dst = (entries, targets)[which]
        pltpu.make_async_copy(dst.at[t], dst.at[t], entry_recv.at[which, t]).wait()

    direct = ((0, not_first, first), (1, not_last, last))
    ends = ((0, (side == 0) & not_first, first), (1, (side == 1) & not_last, last))

    def start_entries(t, from_mail):
        for which, away, here in direct if t == 0 else ends:

            @pl.when(away)
            def _():
                entry_copy(which, t, from_mail).start()

            @pl.when(here)
            def _():
                entry_local(which, t, from_mail).start()

    start_entries(0, 0)

    @pl.when(side == 0)
    def _():
        mail_copy(target_hbm).start()

    @pl.when(side == 1)
    def _():
        mail_copy(entry_hbm).start()

    def columns(j):
        return pl.ds(pl.multiple_of(j * cut, 128), cut)

    def half_columns(j, part):
        half = 1 - py if part == 0 else py
        return pl.ds(pl.multiple_of(j * cut + half * share, 128), share)

    def spread(refs, slot, j, part, src=None):
        held, dst, send_sem, recv_sem = refs
        src = held if src is None else src
        index = slot * 2 + part

        @pl.when(j != px)
        def _():
            pltpu.make_async_remote_copy(
                src_ref=src.at[slot, :, half_columns(j, part)],
                dst_ref=dst.at[px, slot, :, half_columns(0, part)],
                send_sem=send_sem.at[index, j],
                recv_sem=recv_sem.at[px, index],
                device_id={"dp": j * 2 + py},
                device_id_type=MESH,
            ).start()

        @pl.when(j == px)
        def _():
            pltpu.make_async_copy(
                src.at[slot, :, half_columns(j, part)],
                dst.at[px, slot, :, half_columns(0, part)],
                recv_sem.at[px, index],
            ).start()

    def spread_all(refs, slot, part, src=None):
        for k in range(ring):
            spread(refs, slot, lax.rem(px + k, ring), part, src)

    def spread_wait(refs, part):
        src, dst, send_sem, recv_sem = refs

        def one(i, c):
            slot, k = i // ring, i % ring
            index = slot * 2 + part

            @pl.when(k != px)
            def _():
                copy = pltpu.make_async_remote_copy(
                    src_ref=src.at[slot, :, half_columns(k, part)],
                    dst_ref=dst.at[k, slot, :, half_columns(0, part)],
                    send_sem=send_sem.at[index, k],
                    recv_sem=recv_sem.at[k, index],
                    device_id={"dp": k * 2 + py},
                    device_id_type=MESH,
                )
                copy.wait_recv()
                copy.wait_send()

            @pl.when(k == px)
            def _():
                pltpu.make_async_copy(
                    src.at[slot, :, half_columns(k, part)],
                    dst.at[k, slot, :, half_columns(0, part)],
                    recv_sem.at[k, index],
                ).wait()

            return c

        lax.fori_loop(0, ring * TICKS, one, 0)

    x_refs = (inputs.at[1], x_gather, x_send_sem, x_recv_sem)
    g_refs = (g_all, g_gather, g_send_sem, g_recv_sem)

    @pl.when(not_last)
    def _():
        for slot in range(TICKS):
            spread_all(x_refs, slot, 0, act_hbm)

    blocks = act_exps.shape[-1]

    def expand(exps, rows, limits, t):
        scale = jnp.exp2(exps[rows[0, t]].astype(F32) + 4.0)
        for j in range(ring):
            limits[t, :, j * cut : (j + 1) * cut] = jnp.concatenate(
                [
                    jnp.broadcast_to(scale[:, b : b + 1], (ROWS, 128))
                    for b in range(j * blocks // ring, (j + 1) * blocks // ring)
                ],
                axis=1,
            ).astype(BF16)

    def expand_forward(t):
        expand(act_exps, fwd_rows, lim_act, t)

    def expand_backward(t):
        expand(grad_exps, bwd_rows, lim_grad, t)

    for i in (6, 7, 9, 10):
        loads[i].wait()

    @pl.when((s % 2 == 1) | last)
    def _():
        expand_forward(0)

    @pl.when((s % 2 == 0) & not_last)
    def _():
        expand_backward(0)

    loads[1].wait()
    loads[8].wait()

    def fold(j, c):
        wg[:, columns(j)] = (
            w_in[:, columns(j)].astype(F32) * gain_ref[:, columns(j)].astype(F32)
        ).astype(BF16)
        return c

    lax.fori_loop(0, ring, fold, 0)

    def pass_entries():
        start_entries(1, 0)
        mail_copy(target_hbm).wait()
        start_entries(1, 1)

    @pl.when(last)
    def _():
        pass_entries()
    loads[0].wait()

    def y_copy(t, j):
        return pltpu.make_async_remote_copy(
            src_ref=y_send.at[t, :, columns(j)],
            dst_ref=y_recv.at[t, :, columns(j)],
            send_sem=y_send_sem.at[t, j],
            recv_sem=y_recv_sem.at[t, j],
            device_id={"section": s + 1},
            device_id_type=MESH,
        )

    def d_copy(t, j):
        return pltpu.make_async_remote_copy(
            src_ref=d_send.at[t, :, columns(j)],
            dst_ref=d_recv.at[t, :, columns(j)],
            send_sem=d_send_sem.at[t, j],
            recv_sem=d_recv_sem.at[t, j],
            device_id={"section": s - 1},
            device_id_type=MESH,
        )

    def scaled(cache, limit, code):
        return (
            cache.astype(F32) + limit.astype(F32) * 0.0625 * code.astype(F32)
        ).astype(BF16)

    def clipped(cache, limit, value):
        return jnp.minimum(jnp.maximum(value, cache - limit), cache + limit)

    def forward(t):
        row = fwd_rows[0, t]

        @pl.when(first)
        def _():
            entry_wait(0, t)
            if t > 0:
                y_recv[t - 1] = scaled(act[row], lim_act[t], entries[t])
                lim_act[t] = jnp.full((ROWS, width), OPEN, BF16)

        def take(j, c):
            total, u = c
            at = columns(j)
            cache, limit = act[row, :, at], lim_act[t, :, at]
            if t == 0:

                @pl.when(first)
                def _():
                    x_now[:, at] = scaled(cache, limit, entries[t, :, at])

                @pl.when(not_first)
                def _():
                    x_now[:, at] = scaled(cache, limit, fwd_code[:, at])

                x = x_now[:, at]
            else:

                @pl.when(not_first)
                def _():
                    y_copy(t - 1, j).wait_recv()

                x = clipped(cache, limit, y_recv[t - 1, :, at])
                x_now[:, at] = x

            total = total + lane_sums(x)
            u = u + dot_last(x, wg[:, at])

            @pl.when(last)
            def _():
                inputs[1, t, :, at] = x
                spread(x_refs, t, j, 0)
                spread(x_refs, t, j, 1)

            return total, u

        total, u = lax.fori_loop(
            0,
            ring,
            take,
            (jnp.zeros((ROWS, 128), F32), jnp.zeros((ROWS, w_in.shape[0]), F32)),
        )
        total = jnp.sum(total, axis=1, keepdims=True)
        r = lax.rsqrt(total * inv_width + 1e-05)
        u = u * r
        a = gelu(u).astype(BF16)

        @pl.when(last)
        def _():
            u_back[t] = u
            r_back[t] = jnp.broadcast_to(r, (ROWS, 128))
            a_back[t] = a
            slope_back[t] = gelu_slope(u)
            entry_wait(1, t)

        def give(j, c):
            at = columns(j)
            y = x_now[:, at].astype(F32) + dot_plain(a, w_out[:, at])
            y_send[t, :, at] = y.astype(BF16)
            if t < TICKS - 1:

                @pl.when(not_last)
                def _():
                    y_copy(t, j).start()

            @pl.when(last)
            def _():
                g = (y - targets[t, :, at].astype(F32)).astype(BF16)
                if t == 0:
                    g_all[t, :, at] = g
                else:
                    d_recv[t - 1, :, at] = g

            return c

        lax.fori_loop(0, ring, give, 0)
        if t == TICKS - 1:
            pltpu.make_async_copy(y_send.at[t], fwd_out, out_sem.at[0]).start()

    def prepare_backward():
        def take(j, c):
            total, u = c
            at = columns(j)
            x = inputs[0, :, :, at].reshape(TICKS * ROWS, cut)
            return total + lane_sums(x), u + dot_last(x, wg[:, at])

        total, u = lax.fori_loop(
            0,
            ring,
            take,
            (
                jnp.zeros((TICKS * ROWS, 128), F32),
                jnp.zeros((TICKS * ROWS, w_in.shape[0]), F32),
            ),
        )
        total = jnp.sum(total, axis=1, keepdims=True)
        r = lax.rsqrt(total * inv_width + 1e-05)
        u = u * r
        slope_back[...] = gelu_slope(u).reshape(slope_back.shape)
        u_back[...] = u.reshape(u_back.shape)
        r_back[...] = jnp.broadcast_to(r, (TICKS * ROWS, 128)).reshape(r_back.shape)
        a_back[...] = gelu(u).astype(BF16).reshape(a_back.shape)

    def spread_later(t):
        for slot in ((), (0,), (1,), (2, 3))[t]:
            spread_all(g_refs, slot, 1)

        @pl.when(not_last)
        def _():
            for slot in ((0,), (1,), (2,), (3,))[t]:
                spread_all(x_refs, slot, 1, act_hbm)

    def backward_take(t):
        row = bwd_rows[0, t]
        used = jnp.where(last, t, row)

        def take(j, c):
            at = columns(j)

            cache, limit = grad[row, :, at], lim_grad[t, :, at]
            if t == 0:

                @pl.when(not_last)
                def _():
                    g_all[t, :, at] = scaled(cache, limit, bwd_code[:, at])

                g = g_all[t, :, at]
            else:

                @pl.when(not_last)
                def _():
                    d_copy(t - 1, j).wait_recv()

                g = clipped(cache, limit, d_recv[t - 1, :, at])
                g_all[t, :, at] = g
            if t < TICKS - 1:
                spread(g_refs, t, j, 0)
            return c + dot_last(g, w_out[:, at])

        d_active = lax.fori_loop(
            0, ring, take, jnp.zeros((ROWS, w_in.shape[0]), F32)
        )
        if t < TICKS - 1:
            spread_later(t)
        u = u_back[used]
        r = r_back[used][:, :1]
        du = d_active * slope_back[used]
        shift = r * r * (jnp.sum(du * u, axis=1, keepdims=True) * inv_width)
        du_tick[t] = (du * r).astype(BF16)
        factors[1, t] = a_back[used]
        return used, r, shift, du.astype(BF16)

    def backward_give(t, held):
        used, r, shift, du = held

        def give(j, c):
            at = columns(j)
            dx = (
                g_all[t, :, at].astype(F32)
                + r * dot_plain(du, wg[:, at])
                - inputs[x_from, used, :, at].astype(F32) * shift
            )
            d_send[t, :, at] = dx.astype(BF16)
            if t < TICKS - 1:

                @pl.when(not_first)
                def _():
                    d_copy(t, j).start()

            return c

        lax.fori_loop(0, ring, give, 0)
        if t == TICKS - 1:
            pltpu.make_async_copy(d_send.at[t], bwd_out, out_sem.at[1]).start()

    def factor_copy(to, frm):
        return pltpu.make_async_remote_copy(
            src_ref=factors,
            dst_ref=f_gather.at[frm],
            send_sem=f_send_sem.at[to],
            recv_sem=f_recv_sem.at[frm],
            device_id={"dp": to * 2 + py},
            device_id_type=MESH,
        )

    def backward(t):
        backward_give(t, backward_take(t))

    def send_factors():
        used = [jnp.where(last, t, bwd_rows[0, t]) for t in range(TICKS)]
        for q in range(TICKS):
            at = 0
            for t in range(1, TICKS):
                at = jnp.where(used[t] == q, t, at)
            factors[0, q] = du_tick[at]
        for k in range(1, ring):
            factor_copy(lax.rem(px + k, ring), px).start()
        pltpu.make_async_copy(factors, f_gather.at[px], f_recv_sem.at[px]).start()

    rows = ring * TICKS * ROWS
    win = w_in.shape[0]

    def product(which, half):
        at = pl.ds(pl.multiple_of(half * share, 128), share)
        data = (x_gather, g_gather)[which]
        return dot_first(
            f_gather[:, which].reshape(rows, win),
            data[:, :, :, at].reshape(rows, share),
        )

    def swap(which):
        return pltpu.make_async_remote_copy(
            src_ref=p_send.at[which],
            dst_ref=p_recv.at[which],
            send_sem=p_send_sem.at[which],
            recv_sem=p_recv_sem.at[which],
            device_id={"dp": mate},
            device_id_type=MESH,
        )

    def give_product(which):
        p_send[which] = product(which, 1 - py).astype(BF16)
        swap(which).start()

    def spread_last_gradient():
        spread_all(g_refs, TICKS - 1, 0)
        spread_later(TICKS - 1)

    def first_products():
        pltpu.make_async_copy(factors, f_gather.at[px], f_recv_sem.at[px]).wait()
        for k in range(1, ring):
            other = lax.rem(px + k, ring)
            factor_copy(other, other).wait()
        spread_wait(x_refs, 0)
        give_product(0)

    def second_products():
        spread_wait(g_refs, 0)
        give_product(1)

    def rest_of_limits():
        def one(t, c):
            expand_forward(t)
            expand_backward(t)
            return c

        lax.fori_loop(1, TICKS, one, 0)

        @pl.when(last)
        def _():
            for t in range(1, TICKS):
                lim_grad[t] = jnp.full((ROWS, width), OPEN, BF16)

    def more_entries(t):
        start_entries(t, 0)
        start_entries(t, 1)

    @pl.when(last)
    def _():
        for i in (2, 3, 4, 5):
            loads[i].wait()
        forward(0)
        backward(0)
        more_entries(2)
        more_entries(3)
        rest_of_limits()
        for t in range(1, TICKS - 1):
            forward(t)
            backward(t)
        forward(TICKS - 1)
        held = backward_take(TICKS - 1)
        send_factors()
        spread_last_gradient()
        backward_give(TICKS - 1, held)
        first_products()
        second_products()

    @pl.when(not_last)
    def _():
        @pl.when(s % 2 == 1)
        def _():
            for i in (2, 3):
                loads[i].wait()
            forward(0)
            pass_entries()
            for i in (4, 5):
                loads[i].wait()
            prepare_backward()
            expand_backward(0)
            backward(0)

        @pl.when(s % 2 == 0)
        def _():
            prepare_backward()
            for i in (4, 5, 3):
                loads[i].wait()
            backward(0)
            pass_entries()
            loads[2].wait()
            expand_forward(0)
            forward(0)

        more_entries(2)
        more_entries(3)
        rest_of_limits()

        @pl.when(s % 2 == 1)
        def _():
            forward(1)
            backward(1)

        @pl.when(s % 2 == 0)
        def _():
            backward(1)
            forward(1)

        backward(2)
        forward(2)

        @pl.when(s % 2 == 1)
        def _():
            forward(TICKS - 1)

        held = backward_take(TICKS - 1)
        send_factors()
        spread_last_gradient()
        backward_give(TICKS - 1, held)
        first_products()
        second_products()

        @pl.when(s % 2 == 0)
        def _():
            forward(TICKS - 1)


    factor = 1.0 / (TICKS * replicas)
    at = pl.ds(pl.multiple_of(p * share, 128), share)
    spread_wait(x_refs, 1)
    own = product(0, py)
    swap(0).wait()
    total = own + p_recv[0].astype(F32)
    gw_in_out[...] = (total * (gain_ref[:, at].astype(F32) * factor)).astype(BF16)
    ggain_out[...] = (
        jnp.sum(total * w_in[:, at].astype(F32), axis=0, keepdims=True) * factor
    )
    spread_wait(g_refs, 1)
    own = product(1, py)
    swap(1).wait()
    gw_out_out[...] = ((own + p_recv[1].astype(F32)) * factor).astype(BF16)

    for t in range(TICKS):
        for which, away, _ in direct if t == 0 else ends:

            @pl.when(away)
            def _():
                entry_copy(which, t, 0).wait_send()
                if t > 0:
                    entry_copy(which, t, 1).wait_send()

    for t in range(TICKS - 1):
        for j in range(ring):

            @pl.when(not_last)
            def _():
                y_copy(t, j).wait_send()

            @pl.when(not_first)
            def _():
                d_copy(t, j).wait_send()

    pltpu.make_async_copy(y_send.at[TICKS - 1], fwd_out, out_sem.at[0]).wait()
    pltpu.make_async_copy(d_send.at[TICKS - 1], bwd_out, out_sem.at[1]).wait()


def hand_over(*refs):
    sources, results, held, sem = refs[:5], refs[5:10], refs[10:15], refs[15]
    takes = [
        pltpu.make_async_copy(src, mid, sem.at[0, i])
        for i, (src, mid) in enumerate(zip(sources, held))
    ]
    gives = [
        pltpu.make_async_copy(mid, dst, sem.at[1, i])
        for i, (mid, dst) in enumerate(zip(held, results))
    ]
    for take in takes:
        take.start()
    for take, give in zip(takes, gives):
        take.wait()
        give.start()
    for give in gives:
        give.wait()


def solution(mesh):
    sections = mesh.shape["section"]
    replicas = mesh.shape["dp"]

    def body(
        entry_codes,
        loss_target,
        fwd_inflow,
        bwd_inflow,
        act_cache,
        act_exps,
        grad_cache,
        grad_exps,
        fwd_rows,
        bwd_rows,
        norm_gain,
        w_in,
        w_out,
    ):
        win, width = w_in.shape[1:]
        ring = replicas // 2
        cut = width // ring
        share = width // replicas
        blocks = act_exps.shape[-1]
        full = (ROWS, width)
        dma = pltpu.SemaphoreType.DMA
        hbm = pl.BlockSpec(memory_space=pltpu.HBM)
        vmem = pl.BlockSpec(memory_space=pltpu.VMEM)
        outs = pl.pallas_call(
            functools.partial(kernel, sections, replicas),
            out_shape=(
                jax.ShapeDtypeStruct((win, share), BF16),
                jax.ShapeDtypeStruct((win, share), BF16),
                jax.ShapeDtypeStruct((1, share), F32),
                jax.ShapeDtypeStruct(full, BF16),
                jax.ShapeDtypeStruct(full, BF16),
            ),
            in_specs=[hbm] * 13,
            out_specs=(vmem, vmem, vmem, hbm, hbm),
            scratch_shapes=[
                pltpu.SMEM((1, TICKS), jnp.int32),
                pltpu.SMEM((1, TICKS), jnp.int32),
                pltpu.VMEM((1, width), BF16),
                pltpu.VMEM((TICKS, ROWS, blocks), jnp.int32),
                pltpu.VMEM((TICKS, ROWS, blocks), jnp.int32),
                pltpu.VMEM((2, TICKS) + full, BF16),
                pltpu.VMEM((TICKS,) + full, BF16),
                pltpu.VMEM((win, width), BF16),
                pltpu.VMEM((win, width), BF16),
                pltpu.VMEM((win, width), BF16),
                pltpu.VMEM(full, BF16),
                pltpu.VMEM(full, BF16),
                pltpu.VMEM((TICKS,) + full, BF16),
                pltpu.VMEM((TICKS,) + full, BF16),
                pltpu.VMEM((TICKS,) + full, BF16),
                pltpu.VMEM((TICKS,) + full, BF16),
                pltpu.VMEM(full, BF16),
                pltpu.VMEM((TICKS,) + full, BF16),
                pltpu.VMEM((TICKS,) + full, BF16),
                pltpu.VMEM((TICKS - 1,) + full, BF16),
                pltpu.VMEM((TICKS,) + full, BF16),
                pltpu.VMEM((TICKS - 1,) + full, BF16),
                pltpu.VMEM((TICKS, ROWS, win), F32),
                pltpu.VMEM((TICKS, ROWS, win), F32),
                pltpu.VMEM((TICKS, ROWS, 128), F32),
                pltpu.VMEM((TICKS, ROWS, win), BF16),
                pltpu.VMEM((TICKS, ROWS, win), BF16),
                pltpu.VMEM((2, TICKS, ROWS, win), BF16),
                pltpu.VMEM((ring, TICKS, ROWS, cut), BF16),
                pltpu.VMEM((ring, TICKS, ROWS, cut), BF16),
                pltpu.VMEM((ring, 2, TICKS, ROWS, win), BF16),
                pltpu.VMEM((2, win, share), BF16),
                pltpu.VMEM((2, win, share), BF16),
                dma((11,)),
                pltpu.VMEM((TICKS, ROWS, width // sections), BF16),
                dma((2,)),
                dma((2, TICKS)),
                dma((2, TICKS)),
                dma((TICKS - 1, ring)),
                dma((TICKS - 1, ring)),
                dma((TICKS - 1, ring)),
                dma((TICKS - 1, ring)),
                dma((2 * TICKS, ring)),
                dma((ring, 2 * TICKS)),
                dma((2 * TICKS, ring)),
                dma((ring, 2 * TICKS)),
                dma((ring,)),
                dma((ring,)),
                dma((2,)),
                dma((2,)),
                dma((2,)),
            ],
            compiler_params=pltpu.CompilerParams(
                collective_id=0,
                has_side_effects=True,
                vmem_limit_bytes=VMEM_BYTES,
            ),
        )(
            fwd_rows,
            bwd_rows,
            norm_gain,
            act_exps[0],
            grad_exps[0],
            entry_codes,
            loss_target,
            fwd_inflow[0],
            bwd_inflow[0],
            act_cache[0],
            grad_cache[0],
            w_in[0],
            w_out[0],
        )
        gw_in, gw_out, ggain, fwd_last, bwd_last = pl.pallas_call(
            hand_over,
            out_shape=tuple(jax.ShapeDtypeStruct(o.shape, o.dtype) for o in outs),
            in_specs=[pl.BlockSpec(memory_space=pl.ANY)] * 5,
            out_specs=(hbm,) * 5,
            scratch_shapes=[pltpu.VMEM(o.shape, o.dtype) for o in outs] + [dma((2, 5))],
            compiler_params=pltpu.CompilerParams(vmem_limit_bytes=VMEM_BYTES),
        )(*outs)
        return gw_in[None], gw_out[None], ggain, fwd_last[None], bwd_last[None]

    return jax.shard_map(
        body,
        mesh=mesh,
        in_specs=(
            P(None, "dp", "section"),
            P(None, "dp", "section"),
            P("section", "dp", None),
            P("section", "dp", None),
            P("section", "dp", None, None),
            P("section", "dp", None, None),
            P("section", "dp", None, None),
            P("section", "dp", None, None),
            P("section", "dp"),
            P("section", "dp"),
            P("section", None),
            P("section", None, None),
            P("section", None, None),
        ),
        out_specs=(
            P("section", None, "dp"),
            P("section", None, "dp"),
            P("section", "dp"),
            P("section", "dp", None),
            P("section", "dp", None),
        ),
        check_vma=False,
    )
```
